256 devices in a mesh: src: 128 (over x, z, y), frm: 2 (over core).
Axes of the slice: x: 4, y: 4, z: 8, core: 2. Of those that a mesh axis runs over, the one named last changes fastest.
Arguments:
- measured: float32 [512, 256], P(None, 'frm'), may hold values from -4 to 4
- lead_field: bfloat16 [512, 524288], P(None, 'src'), may hold values from -0.0078125 to 0.0078125
- depth: float32 [524288], P('src'), may hold values from 0.5 to 2
- coefficients: float32 [524288, 8, 64], P('src', 'frm'), may hold values from -1.2 to 1.2
- offsets: int32 [8], P('frm'), may hold values from 0 to 240, as said below
- group_ids: int32 [524288], P('src'), may hold values from 0 to 255, as said below
Outputs:
- estimate: float32 [524288, 8, 64], P('src', 'frm')
- residual: float32 [512, 256], P(None, 'frm')
The draws below stay inside these ranges and needn't reach their ends.
Inputs may be any that keep to these rules, and one draw needn't show every extreme that they name: offsets[f] lies between 32 f and 32 f + 16; one frame takes no shift and one the full 32 // 2. `group_ids`: each of the 256 group ids names exactly 2048 sources, which follow one another in circular order of the sources.
All inputs are finite; a program needn't handle non-finite values.
Results may differ from the reference program's by a relative error of at most 0.0019.
Values may be sent and summed in bfloat16 or wider, within the bound.
No kernel may reach another device: no remote copies, remote signals or barrier semaphores. Data moves between devices by JAX's collectives and lax.ppermute only.
A program may use at most 64 MiB of HBM per device.

```python
import math
import jax
import jax.numpy as jnp
from jax import lax

S = 512
K = 64
HOP = 32
FRAMES = 8
GROUP = 2048
ITERS = 3
NSRC = 524288
NT = 256
NGROUP = 256


def group_shift(key):
    return jax.random.randint(jax.random.fold_in(key, 40), (), 0, GROUP, dtype=jnp.int32)


def draw_offsets(key, part):
    key = jax.random.fold_in(key, 11)
    jitter = jax.random.randint(key, (FRAMES,), 0, HOP // 2 + 1, dtype=jnp.int32)
    order = jax.random.permutation(jax.random.fold_in(key, 1), FRAMES)
    jitter = jitter.at[order[0]].set(HOP // 2).at[order[1]].set(0)
    return jnp.arange(FRAMES, dtype=jnp.int32) * HOP + jitter


def draw_group_ids(key, part):
    first = group_shift(key)
    return (jnp.arange(NSRC, dtype=jnp.int32) + first) // GROUP % NGROUP


def draw_coefficients(key, part):
    first = group_shift(key)
    key = jax.random.fold_in(key, 13)
    owner = (jnp.arange(NSRC, dtype=jnp.int32) + first) // GROUP % NGROUP
    quiet_count = max(1, NGROUP // 4)
    ranking = jax.random.permutation(jax.random.fold_in(key, 1), NGROUP)
    quiet = (ranking < quiet_count)[owner]
    level = jnp.where(quiet, jnp.float32(0.02), jnp.float32(0.2))
    noise = jax.random.normal(jax.random.fold_in(key, 2), (NSRC, FRAMES, K), jnp.float32)
    noise = jnp.clip(noise, -6.0, 6.0)
    return level[:, None, None] * noise


def level_of(stream_key, extent, shards, low, largest):
    factor_of = 1.0
    for axis_at, shards_of in shards:
        steps = jax.random.uniform(jax.random.fold_in(jax.random.fold_in(stream_key, 6), axis_at), (shards_of,), jnp.float32, low / len(shards), largest / len(shards))
        factor_of = factor_of * jnp.repeat(jnp.exp(steps), extent[axis_at] // shards_of).reshape((-1,) + (1,) * (len(extent) - 1 - axis_at))
    return factor_of


def gaussian(rng, dims, scale, bound, pieces=(), held_as=jnp.bfloat16):
    drawn = scale * jax.random.normal(rng, dims, jnp.float32)
    if pieces:
        drawn = drawn * level_of(rng, dims, pieces, -0.22, 0.18)
    return jnp.clip(drawn, -bound, bound).astype(held_as)


def setup_inputs(seed: int = 0) -> dict:
    key_list = jax.random.split(jax.random.key(seed), 7)
    measured = gaussian(key_list[0], (S, NT), 0.5, 4.0, ((1, 2),), jnp.float32)
    lead_field = gaussian(key_list[1], (S, NSRC), NSRC ** -0.5, 0.0078125, ((1, 128),))
    depth = jnp.clip(jnp.exp(math.log(2.0) - 1.3862944 * jax.random.uniform(key_list[2], (NSRC,), jnp.float32) ** level_of(key_list[2], (NSRC,), ((0, 128),), -0.2, 0.2)), 0.5, 2.0)
    coefficients = draw_coefficients(jax.random.fold_in(key_list[6], 71), 0)
    offsets = draw_offsets(jax.random.fold_in(key_list[6], 71), 0)
    group_ids = draw_group_ids(jax.random.fold_in(key_list[6], 71), 0)
    return dict(measured=measured, lead_field=lead_field, depth=depth, coefficients=coefficients, offsets=offsets, group_ids=group_ids)


step_size = 0.5
shrink_one = 0.05
group_weight = 0.03
epsilon = 1e-06

def atoms(offsets):
    samples = jnp.arange(NT, dtype=jnp.int32)
    delay = (samples[None, None, :] - offsets[:, None, None]) % NT
    inside = delay < K
    delayf = delay.astype(jnp.float32)
    freq = jnp.arange(K, dtype=jnp.int32).astype(jnp.float32)[None, :, None]
    window = jnp.sin(jnp.pi * (delayf + 0.5) / K)
    basis = jnp.sqrt(2.0 / K) * jnp.cos(jnp.pi * (freq + 0.5) * (delayf + 0.5) / K)
    table = jnp.where(inside, window * basis, jnp.float32(0.0))
    return table.reshape(FRAMES * K, NT)

def window_basis():
    delayf = jnp.arange(K, dtype=jnp.int32).astype(jnp.float32)[None, :]
    freq = jnp.arange(K, dtype=jnp.int32).astype(jnp.float32)[:, None]
    window = jnp.sin(jnp.pi * (delayf + 0.5) / K)
    basis = jnp.sqrt(2.0 / K) * jnp.cos(jnp.pi * (freq + 0.5) * (delayf + 0.5) / K)
    return window * basis

def placement(offsets):
    samples = jnp.arange(NT, dtype=jnp.int32)
    delay = (samples[None, None, :] - offsets[:, None, None]) % NT
    position = jnp.arange(K, dtype=jnp.int32)[None, :, None]
    return (delay == position).astype(jnp.float32).reshape(FRAMES * K, NT)

def reference(measured, lead_field, depth, coefficients, offsets, group_ids):
    table = atoms(offsets)
    wave_table = window_basis()
    placing = placement(offsets)
    ngroups = NSRC // GROUP
    tau = group_weight * (GROUP * FRAMES * K) ** 0.5
    state = coefficients.reshape(NSRC, FRAMES * K)
    residual = measured
    for iteration in range(ITERS):
        waveforms = jnp.einsum('sfk,kt->sft', state.reshape(NSRC, FRAMES, K), wave_table, precision=lax.Precision.HIGHEST)
        weighted = (depth[:, None, None] * waveforms).astype(jnp.bfloat16).reshape(NSRC, FRAMES * K)
        sensor_frames = jnp.dot(lead_field, weighted, preferred_element_type=jnp.float32)
        residual = measured - jnp.dot(sensor_frames, placing, precision=lax.Precision.HIGHEST)
        residual_b = residual.astype(jnp.bfloat16)
        back = depth[:, None] * jnp.dot(lead_field.T, residual_b, preferred_element_type=jnp.float32)
        gradient = jnp.dot(back, table.T, precision=lax.Precision.HIGHEST)
        moved = state + step_size * gradient
        shrunk = jnp.sign(moved) * jnp.maximum(jnp.abs(moved) - shrink_one, 0.0)
        power = jax.ops.segment_sum(lax.optimization_barrier(jnp.sum(shrunk * shrunk, axis=1)), group_ids, ngroups)
        scale = jnp.maximum(0.0, 1.0 - tau / jnp.sqrt(power + epsilon))
        state = shrunk * scale[group_ids][:, None]
    return (state.reshape(NSRC, FRAMES, K), residual)
```

```python
import functools

import jax
import jax.numpy as jnp
from jax import lax
from jax.experimental import pallas as pl
from jax.experimental.pallas import tpu as pltpu
from jax.sharding import PartitionSpec as P

K = 64
GROUP = 2048
ITERS = 3
LANES = 128
BLOCK = 512

step_size = 0.5
shrink_one = 0.05
group_weight = 0.03
epsilon = 1e-06

F32 = jnp.float32
BF16 = jnp.bfloat16
HIGHEST = lax.Precision.HIGHEST
EVERY = ("src", "frm")
PARAMS = pltpu.CompilerParams(vmem_limit_bytes=48 * 1024 * 1024)


def atoms_by_owner(offsets, samples, total):
    delay = (samples[None, None, :] - offsets[:, None, None]) % total
    delayf = delay.astype(F32)
    freq = jnp.arange(K, dtype=jnp.int32).astype(F32)[None, :, None]
    window = jnp.sin(jnp.pi * (delayf + 0.5) / K)
    basis = jnp.sqrt(2.0 / K) * jnp.cos(jnp.pi * (freq + 0.5) * (delayf + 0.5) / K)
    table = jnp.where(delay < K, window * basis, F32(0.0))
    return table.reshape(offsets.shape[0] * K, samples.shape[0])


def split(x):
    high = x.astype(BF16)
    return high, (x - high.astype(F32)).astype(BF16)


def against_sources(high, low, lead):
    both = jnp.concatenate([high, low], axis=0)
    product = lax.dot_general(both, lead, (((1,), (1,)), ((), ())), preferred_element_type=F32)
    rows = high.shape[0]
    return product[:rows] + product[rows:]


def to_samples(atoms_t, sums):
    return jnp.dot(atoms_t, sums, precision=HIGHEST, preferred_element_type=F32)


def first_kernel(coef_ref, depth_ref, lead_ref, atoms_t_ref, state_ref, out_ref, acc_ref):
    step = pl.program_id(0)
    frames = coef_ref.shape[1]
    for f in range(frames):
        state_ref[f * K : (f + 1) * K, :] = coef_ref[:, f, :].T
    high, low = split(state_ref[...] * depth_ref[...])
    part = against_sources(high, low, lead_ref[...])

    @pl.when(step == 0)
    def _():
        acc_ref[...] = part

    @pl.when(step != 0)
    def _():
        acc_ref[...] += part

    @pl.when(step == pl.num_programs(0) - 1)
    def _():
        out_ref[...] = to_samples(atoms_t_ref[...], acc_ref[...]).astype(BF16)


def forward_kernel(state_ref, weight_ref, lead_ref, atoms_t_ref, out_ref, acc_ref):
    step = pl.program_id(0)
    high, low = split(state_ref[...] * weight_ref[...])
    part = against_sources(high, low, lead_ref[...])

    @pl.when(step == 0)
    def _():
        acc_ref[...] = part

    @pl.when(step != 0)
    def _():
        acc_ref[...] += part

    @pl.when(step == pl.num_programs(0) - 1)
    def _():
        out_ref[...] = to_samples(atoms_t_ref[...], acc_ref[...]).astype(BF16)


def backward_kernel(
    edge_ref, res_ref, atoms_ref, state_ref, scale_ref, depth_ref, lead_ref, new_ref, power_ref, turned_ref
):
    step = pl.program_id(0)
    coefs, block = state_ref.shape

    @pl.when(step == 0)
    def _():
        turned = jnp.dot(
            atoms_ref[...], res_ref[...].astype(F32), precision=HIGHEST, preferred_element_type=F32
        )
        high, low = split(turned)
        turned_ref[:coefs, :] = high
        turned_ref[coefs:, :] = low
        power_ref[...] = jnp.zeros_like(power_ref)

    both = jnp.dot(turned_ref[...], lead_ref[...], preferred_element_type=F32)
    gradient = both[:coefs] + both[coefs:]
    moved = state_ref[...] * scale_ref[...] + (step_size * depth_ref[...]) * gradient
    shrunk = moved - jnp.clip(moved, -shrink_one, shrink_one)
    new_ref[...] = shrunk
    squares = jnp.sum(shrunk * shrunk, axis=0, keepdims=True)
    source = step * block + lax.broadcasted_iota(jnp.int32, (1, block), 1)
    edge = edge_ref[0]
    groups = (source < edge, (source >= edge) & (source < edge + GROUP), source >= edge + GROUP)
    for g, mine in enumerate(groups):
        power_ref[g : g + 1, :] += jnp.sum(jnp.where(mine, squares, 0.0), axis=1, keepdims=True)


def last_kernel(state_ref, scale_ref, out_ref):
    frames = out_ref.shape[1]
    scaled = state_ref[...] * scale_ref[...]
    for f in range(frames):
        out_ref[:, f, :] = scaled[f * K : (f + 1) * K, :].T


def columns(rows, block=BLOCK):
    return pl.BlockSpec((rows, block), lambda i: (0, i))


def whole(*shape):
    return pl.BlockSpec(shape, lambda i: (0,) * len(shape))


def shards(measured, lead_field, depth, coefficients, offsets, group_ids):
    sensors, own_time = measured.shape
    sources = lead_field.shape[1]
    frame_count = coefficients.shape[1]
    src_count, frm_count = lax.axis_size("src"), lax.axis_size("frm")
    devices = src_count * frm_count
    total = own_time * frm_count
    coefs = frame_count * K
    tau = group_weight * (GROUP * frame_count * frm_count * K) ** 0.5
    grid = (sources // BLOCK,)
    tiles = sensors // LANES

    place = jnp.arange(devices, dtype=jnp.int32)
    samples = (place % frm_count) * own_time + place // frm_count
    table = atoms_by_owner(offsets, samples, total)
    table_t = table.T
    own_row = lax.dynamic_slice_in_dim(measured, lax.axis_index("src"), 1, axis=1)
    own_row = own_row.reshape(tiles, LANES)
    depth_row = depth.reshape(1, sources)
    edge = jnp.sum((group_ids == group_ids[0]).astype(jnp.int32))
    source = jnp.arange(sources, dtype=jnp.int32)

    def exchange(rows):
        return lax.all_to_all(rows, EVERY, 0, 0, tiled=True)

    def broadcast(rows):
        return exchange(jnp.broadcast_to(rows[None], (devices,) + rows.shape))

    def owned_residual(predicted):
        arrived = exchange(predicted.reshape(devices, tiles, LANES))
        return own_row - jnp.sum(arrived.astype(F32), axis=0)

    state, predicted = pl.pallas_call(
        first_kernel,
        grid=grid,
        in_specs=[
            pl.BlockSpec((BLOCK, frame_count, K), lambda i: (i, 0, 0)),
            columns(1),
            columns(sensors),
            whole(total, coefs),
        ],
        out_specs=[columns(coefs), whole(total, sensors)],
        out_shape=[
            jax.ShapeDtypeStruct((coefs, sources), F32),
            jax.ShapeDtypeStruct((total, sensors), BF16),
        ],
        scratch_shapes=[pltpu.VMEM((coefs, sensors), F32)],
        compiler_params=PARAMS,
        name="first_forward",
    )(coefficients, depth_row, lead_field, table_t)

    scale_row = jnp.ones((1, sources), F32)
    for iteration in range(ITERS):
        row = owned_residual(predicted)
        if iteration < ITERS - 1:
            everyone = broadcast(row.astype(BF16)).reshape(total, sensors)
        else:
            high = lax.reduce_precision(row, 8, 7)
            both = jnp.concatenate([high, row - high], axis=0).astype(BF16)
            pair = broadcast(both).reshape(devices, 2, tiles, LANES)
            everyone = pair[:, 0].reshape(total, sensors)
            mine = pair.reshape(src_count, frm_count, 2, sensors)
            mine = lax.dynamic_index_in_dim(mine, lax.axis_index("frm"), 1, keepdims=False)
            residual = (mine[:, 0].astype(F32) + mine[:, 1].astype(F32)).T

        state, power = pl.pallas_call(
            backward_kernel,
            grid=grid,
            in_specs=[
                pl.BlockSpec(memory_space=pltpu.SMEM),
                whole(total, sensors),
                whole(coefs, total),
                columns(coefs),
                columns(1),
                columns(1),
                columns(sensors),
            ],
            out_specs=[columns(coefs), whole(8, LANES)],
            out_shape=[
                jax.ShapeDtypeStruct((coefs, sources), F32),
                jax.ShapeDtypeStruct((8, LANES), F32),
            ],
            scratch_shapes=[pltpu.VMEM((2 * coefs, sensors), BF16)],
            compiler_params=PARAMS,
            name="backward",
        )(edge[None], everyone, table, state, scale_row, depth_row, lead_field)

        chip = power + lax.ppermute(power, "frm", [(i, (i + 1) % frm_count) for i in range(frm_count)])
        ahead = [(i, (i + 1) % src_count) for i in range(src_count)]
        behind = [((i + 1) % src_count, i) for i in range(src_count)]
        before = lax.ppermute(chip, "src", ahead)
        after = lax.ppermute(chip, "src", behind)
        sums = jnp.stack([chip[0, 0] + before[2, 0], chip[1, 0], chip[2, 0] + after[0, 0]])
        scale = jnp.maximum(0.0, 1.0 - tau / jnp.sqrt(sums + epsilon))
        scale_row = jnp.where(
            source < edge, scale[0], jnp.where(source < edge + GROUP, scale[1], scale[2])
        )[None, :]
        if iteration < ITERS - 1:
            predicted = pl.pallas_call(
                forward_kernel,
                grid=grid,
                in_specs=[columns(coefs), columns(1), columns(sensors), whole(total, coefs)],
                out_specs=whole(total, sensors),
                out_shape=jax.ShapeDtypeStruct((total, sensors), BF16),
                scratch_shapes=[pltpu.VMEM((coefs, sensors), F32)],
                compiler_params=PARAMS,
                name="forward",
            )(state, depth_row * scale_row, lead_field, table_t)

    estimate = pl.pallas_call(
        last_kernel,
        grid=grid,
        in_specs=[columns(coefs), columns(1)],
        out_specs=pl.BlockSpec((BLOCK, frame_count, K), lambda i: (i, 0, 0)),
        out_shape=jax.ShapeDtypeStruct((sources, frame_count, K), F32),
        compiler_params=PARAMS,
        name="scaled_estimate",
    )(state, scale_row)
    return (estimate, residual)


def solution(mesh):
    return jax.shard_map(
        shards,
        mesh=mesh,
        in_specs=(
            P(None, "frm"),
            P(None, "src"),
            P("src"),
            P("src", "frm", None),
            P("frm"),
            P("src"),
        ),
        out_specs=(P("src", "frm", None), P(None, "frm")),
        check_vma=False,
    )
```

```python
import math

import jax
import jax.numpy as jnp
import numpy as np
from jax import lax
from jax.experimental import pallas as pl
from jax.experimental.pallas import tpu as pltpu
from jax.sharding import PartitionSpec as P

K = 64
GROUP = 2048
ITERS = 3
LANES = 128
BLOCK = 512

step_size = 0.5
shrink_one = 0.05
group_weight = 0.03
epsilon = 1e-06

F32 = jnp.float32
BF16 = jnp.bfloat16
HIGHEST = lax.Precision.HIGHEST
PARAMS = pltpu.CompilerParams(vmem_limit_bytes=24 * 1024 * 1024)


def windowed_cosines():
    t = np.arange(K)[:, None] + 0.5
    k = np.arange(K)[None, :] + 0.5
    return (np.sin(np.pi * t / K) * np.sqrt(2.0 / K) * np.cos(np.pi * k * t / K)).astype(np.float32)


def split(x):
    high = x.astype(BF16)
    return high, (x - high.astype(F32)).astype(BF16)


def dot(a, b):
    return jnp.dot(a, b, preferred_element_type=F32)


def dot_t(a, b):
    return lax.dot_general(a, b, (((1,), (1,)), ((), ())), preferred_element_type=F32)


def to_samples(atoms_ref, sums):
    high, low = split(sums)
    return dot(atoms_ref[0], high) + dot(atoms_ref[0], low) + dot(atoms_ref[1], high)


def group_scale(power, tau):
    return jnp.maximum(0.0, 1.0 - tau / jnp.sqrt(power + epsilon))


def first_kernel(
    offsets_ref, place_ref, wave_ref, coef_ref, depth_ref, lead_ref,
    table_ref, table_t_ref, mine_ref, theirs_ref, acc_ref,
):
    step = pl.program_id(0)
    total = table_ref.shape[2]
    own = mine_ref.shape[0]

    @pl.when(step == 0)
    def _():
        acc_ref[...] = jnp.zeros_like(acc_ref)
        wave = wave_ref[...]
        order = lax.broadcasted_iota(jnp.int32, (total, K), 0)
        sample = (order + place_ref[0]) % total
        position = lax.broadcasted_iota(jnp.int32, (total, K), 1)
        for f in range(offsets_ref.shape[0]):
            delay = (sample - offsets_ref[f] + total) % total
            placing = (delay == position).astype(F32)
            part_t = jnp.dot(placing, wave, precision=HIGHEST, preferred_element_type=F32)
            rows = slice(f * K, (f + 1) * K)
            table_t_ref[0, :, rows], table_t_ref[1, :, rows] = split(part_t)
            table_ref[0, rows, :], table_ref[1, rows, :] = split(part_t.T)

    weighted = (coef_ref[...] * depth_ref[...]).astype(BF16)
    acc_ref[...] += dot_t(weighted, lead_ref[...])

    @pl.when(step == pl.num_programs(0) - 1)
    def _():
        samples = to_samples(table_t_ref, acc_ref[...])
        mine_ref[...] = samples[:own]
        theirs_ref[...] = samples[own:].astype(BF16)


def step_kernel(
    edge_ref, own_ref, other_ref, table_ref, table_t_ref, state_ref, scale_ref, depth_ref, lead_ref,
    new_ref, power_ref, *rest, width, predict,
):
    if predict:
        mine_ref, theirs_ref, turned_ref, rows_ref, acc_ref = rest
    else:
        turned_ref, rows_ref = rest
    step = pl.program_id(0)
    coefs, block = state_ref.shape
    sensors = lead_ref.shape[0]
    tiles = sensors // LANES
    own = table_ref.shape[2] // 2

    @pl.when(step == 0)
    def _():
        for h, ref in enumerate((own_ref, other_ref)):
            rows_ref[h, : ref.shape[0]] = ref[...].astype(F32)
        for t in range(tiles):
            lanes = slice(t * LANES, (t + 1) * LANES)
            turned = jnp.zeros((coefs, LANES), F32)
            for h, apart in enumerate((width, tiles)):
                samples = rows_ref[h, pl.ds(t, own, stride=apart), :].astype(BF16)
                cols = slice(h * own, (h + 1) * own)
                turned += dot(table_ref[0, :, cols], samples) + dot(table_ref[1, :, cols], samples)
            turned_ref[:coefs, lanes], turned_ref[coefs:, lanes] = split(turned)
        power_ref[...] = jnp.zeros_like(power_ref)
        if predict:
            acc_ref[...] = jnp.zeros_like(acc_ref)

    lead = lead_ref[...]
    both = dot(turned_ref[...], lead)
    first = step * block
    source = first + lax.broadcasted_iota(jnp.int32, (1, block), 1)
    start = edge_ref[0]
    end = start + GROUP
    scale = jnp.where(
        source < start, scale_ref[0:1, 0:1], jnp.where(source < end, scale_ref[1:2, 0:1], scale_ref[2:3, 0:1])
    )
    depth = depth_ref[...]
    moved = state_ref[...] * scale + (step_size * depth) * (both[:coefs] + both[coefs:])
    shrunk = moved - jnp.clip(moved, -shrink_one, shrink_one)
    new_ref[...] = shrunk
    squares = jnp.sum(shrunk * shrunk, axis=0, keepdims=True)
    groups = (source < start, (source >= start) & (source < end), source >= end)
    for g, inside in enumerate(groups):
        power_ref[g : g + 1, :] += jnp.sum(jnp.where(inside, squares, 0.0), axis=1, keepdims=True)

    if predict:
        weighted = shrunk * depth
        part = (first >= start).astype(jnp.int32) + (first >= end).astype(jnp.int32)
        bound = jnp.where(part == 0, start, jnp.where(part == 1, end, pl.num_programs(0) * block))
        before = source < bound
        rows = pl.ds(pl.multiple_of(part * coefs, coefs), coefs)
        acc_ref[rows, :] += dot_t(jnp.where(before, weighted, 0.0).astype(BF16), lead)

        @pl.when(bound < first + block)
        def _():
            later = pl.ds(pl.multiple_of((part + 1) * coefs, coefs), coefs)
            acc_ref[later, :] += dot_t(jnp.where(before, 0.0, weighted).astype(BF16), lead)

        @pl.when(step == pl.num_programs(0) - 1)
        def _():
            for g in range(3):
                samples = to_samples(table_t_ref, acc_ref[g * coefs : (g + 1) * coefs, :])
                mine_ref[g * own : (g + 1) * own, :] = samples[:own]
                theirs_ref[g * own : (g + 1) * own, :] = samples[own:].astype(BF16)
            high, low = split(power_ref[...])
            for t in range(tiles):
                lanes = slice(t * LANES, (t + 1) * LANES)
                theirs_ref[3 * own : 3 * own + 16, lanes] = jnp.concatenate([high, low], axis=0)


def first_fold_kernel(mine_ref, theirs_ref, out_ref, rows_ref):
    own = mine_ref.shape[0]
    tiles = mine_ref.shape[1] // LANES
    for t in range(tiles):
        lanes = slice(t * LANES, (t + 1) * LANES)
        rows_ref[pl.ds(t, own, stride=tiles), :] = mine_ref[:, lanes] + theirs_ref[:, lanes].astype(F32)
    out_ref[...] = rows_ref[...].astype(BF16)


def fold_kernel(mine_ref, theirs_ref, power_ref, out_ref, chip_ref, rows_ref, *, tau):
    own = mine_ref.shape[0] // 3
    tiles = mine_ref.shape[1] // LANES
    theirs = theirs_ref[3 * own : 3 * own + 16, :LANES].astype(F32)
    chip = power_ref[...] + theirs[:8] + theirs[8:]
    chip_ref[...] = chip
    middle = group_scale(chip[1:2, :], tau)
    for g, part in enumerate((1, 0, 2)):
        for t in range(tiles):
            lanes = slice(t * LANES, (t + 1) * LANES)
            rows = slice(part * own, (part + 1) * own)
            total = mine_ref[rows, lanes] + theirs_ref[rows, lanes].astype(F32)
            if part == 1:
                total = total * middle
            rows_ref[pl.ds(g * tiles + t, own, stride=16), :] = total
    for g, part in enumerate((0, 2)):
        value = chip[part : part + 1, :]
        high = value.astype(BF16).astype(F32)
        for n, term in enumerate((high, value - high)):
            at = 3 * tiles + 2 * g + n
            rows_ref[pl.ds(at, own, stride=16), :] = jnp.broadcast_to(term, (own, LANES))
    out_ref[...] = rows_ref[...].astype(BF16)


def send_residual(row, out_ref, rows_ref, tiles, last):
    own = out_ref.shape[0] // (2 * tiles if last else tiles)
    if last:
        high = row.astype(BF16).astype(F32)
        row = jnp.concatenate([high, row - high], axis=0)
    out_ref[...] = jnp.concatenate([row.astype(BF16)] * own, axis=0)


def first_owner_kernel(got_ref, measured_ref, out_ref, rows_ref):
    tiles = measured_ref.shape[0]
    senders = got_ref.shape[0] // tiles
    rows_ref[...] = got_ref[...].astype(F32)
    row = [
        measured_ref[t : t + 1, :]
        - jnp.sum(rows_ref[pl.ds(t, senders, stride=tiles), :], axis=0, keepdims=True)
        for t in range(tiles)
    ]
    send_residual(jnp.concatenate(row, axis=0), out_ref, rows_ref, tiles, False)


def owner_kernel(me_ref, got_ref, measured_ref, chip_ref, out_ref, scale_ref, rows_ref, edges_ref, *, tau, last):
    tiles = measured_ref.shape[0]
    senders = got_ref.shape[0] // 16
    rows_ref[...] = got_ref[...].astype(F32)

    def of(k):
        return rows_ref[pl.ds(k, senders, stride=16), :]

    front = of(3 * tiles) + of(3 * tiles + 1)
    back = of(3 * tiles + 2) + of(3 * tiles + 3)
    before = jnp.concatenate([back[senders - 1 :], back[: senders - 1]], axis=0)
    front_scale = group_scale(front + before, tau)
    back_scale = jnp.concatenate([front_scale[1:], front_scale[:1]], axis=0)
    row = []
    for t in range(tiles):
        parts = of(t) + front_scale * of(tiles + t) + back_scale * of(2 * tiles + t)
        row.append(measured_ref[t : t + 1, :] - jnp.sum(parts, axis=0, keepdims=True))
    send_residual(jnp.concatenate(row, axis=0), out_ref, rows_ref, tiles, last)
    edges_ref[0] = front_scale
    edges_ref[1] = back_scale
    me = me_ref[0]
    scale_ref[...] = jnp.zeros_like(scale_ref)
    scale_ref[0:1, :] = edges_ref[0, pl.ds(me, 1), :]
    scale_ref[1:2, :] = group_scale(chip_ref[1:2, :], tau)
    scale_ref[2:3, :] = edges_ref[1, pl.ds(me, 1), :]


def residual_kernel(own_ref, out_ref, rows_ref):
    own = out_ref.shape[1]
    tiles = out_ref.shape[0] // LANES
    rows_ref[...] = own_ref[...].astype(F32)
    for t in range(tiles):
        high = rows_ref[pl.ds(t, own, stride=2 * tiles), :]
        low = rows_ref[pl.ds(tiles + t, own, stride=2 * tiles), :]
        out_ref[t * LANES : (t + 1) * LANES, :] = (high + low).T


def last_kernel(edge_ref, state_ref, chip_ref, before_ref, after_ref, out_ref, *, tau):
    block = state_ref.shape[1]
    source = pl.program_id(0) * block + lax.broadcasted_iota(jnp.int32, (1, block), 1)
    first = group_scale(chip_ref[0:1, 0:1] + before_ref[2:3, 0:1], tau)
    middle = group_scale(chip_ref[1:2, 0:1], tau)
    last = group_scale(chip_ref[2:3, 0:1] + after_ref[0:1, 0:1], tau)
    start = edge_ref[0]
    scale = jnp.where(source < start, first, jnp.where(source < start + GROUP, middle, last))
    out_ref[...] = state_ref[...] * scale


def columns(rows, block=BLOCK):
    return pl.BlockSpec((rows, block), lambda i: (0, i))


def whole(*shape):
    return pl.BlockSpec(shape, lambda i: (0,) * len(shape))


SMEM = pl.BlockSpec(memory_space=pltpu.SMEM)
VMEM = pl.BlockSpec(memory_space=pltpu.VMEM)


def shards(measured, lead_field, depth, coefficients, offsets, group_ids):
    sensors, own = measured.shape
    sources = lead_field.shape[1]
    frames = coefficients.shape[1]
    src_count, frm_count = lax.axis_size("src"), lax.axis_size("frm")
    total = own * frm_count
    coefs = frames * K
    tau = group_weight * math.sqrt(GROUP * frames * frm_count * K)
    grid = (sources // BLOCK,)
    tiles = sensors // LANES
    across = [(i, (i + 1) % frm_count) for i in range(frm_count)]
    ahead = [(i, (i + 1) % src_count) for i in range(src_count)]
    behind = [((i + 1) % src_count, i) for i in range(src_count)]

    me = lax.axis_index("src")
    place = (lax.axis_index("frm") * own)[None]
    own_row = lax.dynamic_slice_in_dim(measured, me, 1, axis=1).reshape(tiles, LANES)
    depth_row = depth.reshape(1, sources)
    edge = jnp.sum((group_ids == group_ids[0]).astype(jnp.int32))[None]

    def struct(dtype, *shape):
        return jax.ShapeDtypeStruct(shape, dtype)

    def call(kernel, name, ins, outs, scratch=()):
        return pl.pallas_call(
            kernel, in_specs=ins, out_specs=[VMEM] * len(outs), out_shape=outs,
            scratch_shapes=list(scratch), compiler_params=PARAMS, name=name,
        )

    def exchange(rows):
        return lax.all_to_all(rows, "src", 0, 0, tiled=True)

    state = coefficients.transpose(1, 2, 0).reshape(coefs, sources)
    table, table_t, mine, theirs = pl.pallas_call(
        first_kernel,
        grid=grid,
        in_specs=[SMEM, SMEM, whole(K, K), columns(coefs), columns(1), columns(sensors)],
        out_specs=[whole(2, coefs, total), whole(2, total, coefs), whole(own, sensors), whole(own, sensors)],
        out_shape=[
            struct(BF16, 2, coefs, total),
            struct(BF16, 2, total, coefs),
            struct(F32, own, sensors),
            struct(BF16, own, sensors),
        ],
        scratch_shapes=[pltpu.VMEM((coefs, sensors), F32)],
        compiler_params=PARAMS,
        name="first_forward",
    )(offsets, place, jnp.asarray(windowed_cosines()), state, depth_row, lead_field)

    folded = call(
        first_fold_kernel,
        "first_fold",
        [VMEM, VMEM],
        [struct(BF16, own * tiles, LANES)],
        [pltpu.VMEM((own * tiles, LANES), F32)],
    )(mine, lax.ppermute(theirs, "frm", across))[0]
    scale = jnp.ones((8, LANES), F32)
    for iteration in range(ITERS):
        last = iteration == ITERS - 1
        got = exchange(folded)
        width = 2 * tiles if last else tiles
        if iteration == 0:
            row = call(
                first_owner_kernel,
                "first_owner",
                [VMEM, VMEM],
                [struct(BF16, own * width, LANES)],
                [pltpu.VMEM((src_count * tiles, LANES), F32)],
            )(got, own_row)[0]
        else:
            row, scale = call(
                lambda *refs, last=last: owner_kernel(*refs, tau=tau, last=last),
                "owner",
                [SMEM, VMEM, VMEM, VMEM],
                [struct(BF16, own * width, LANES), struct(F32, 8, LANES)],
                [pltpu.VMEM((src_count * 16, LANES), F32), pltpu.VMEM((2, src_count, LANES), F32)],
            )(me[None], got, own_row, chip)
        mine = exchange(row)
        send = mine.reshape(own, width, LANES)[:, :tiles].reshape(own * tiles, LANES) if last else mine
        others = lax.ppermute(send, "frm", across)

        outs = [struct(F32, coefs, sources), struct(F32, 8, LANES)]
        out_specs = [columns(coefs), whole(8, LANES)]
        scratch = [pltpu.VMEM((2 * coefs, sensors), BF16), pltpu.VMEM((2, own * width, LANES), F32)]
        if not last:
            outs += [struct(F32, 3 * own, sensors), struct(BF16, 3 * own + 16, sensors)]
            out_specs += [whole(3 * own, sensors), whole(3 * own + 16, sensors)]
            scratch += [pltpu.VMEM((3 * coefs, sensors), F32)]
        results = pl.pallas_call(
            lambda *refs, width=width, last=last: step_kernel(*refs, width=width, predict=not last),
            grid=grid,
            in_specs=[
                SMEM,
                whole(own * width, LANES),
                whole(own * tiles, LANES),
                whole(2, coefs, total),
                whole(2, total, coefs),
                columns(coefs),
                whole(8, LANES),
                columns(1),
                columns(sensors),
            ],
            out_specs=out_specs,
            out_shape=outs,
            scratch_shapes=scratch,
            compiler_params=PARAMS,
            name="step",
        )(edge, mine, others, table, table_t, state, scale, depth_row, lead_field)
        state, power = results[:2]
        if last:
            break
        folded, chip = call(
            lambda *refs: fold_kernel(*refs, tau=tau),
            "fold",
            [VMEM, VMEM, VMEM],
            [struct(BF16, own * 16, LANES), struct(F32, 8, LANES)],
            [pltpu.VMEM((own * 16, LANES), F32)],
        )(results[2], lax.ppermute(results[3], "frm", across), power)

    chip = power + lax.ppermute(power, "frm", across)
    before = lax.ppermute(chip, "src", ahead)
    after = lax.ppermute(chip, "src", behind)
    residual = call(
        residual_kernel,
        "residual",
        [VMEM],
        [struct(F32, sensors, own)],
        [pltpu.VMEM((own * 2 * tiles, LANES), F32)],
    )(mine)[0]
    estimate = pl.pallas_call(
        lambda *refs: last_kernel(*refs, tau=tau),
        grid=grid,
        in_specs=[SMEM, columns(coefs), whole(8, LANES), whole(8, LANES), whole(8, LANES)],
        out_specs=columns(coefs),
        out_shape=struct(F32, coefs, sources),
        compiler_params=PARAMS,
        name="scaled_estimate",
    )(edge, state, chip, before, after)
    return (estimate.reshape(frames, K, sources).transpose(2, 0, 1), residual)


def solution(mesh):
    return jax.shard_map(
        shards,
        mesh=mesh,
        in_specs=(
            P(None, "frm"),
            P(None, "src"),
            P("src"),
            P("src", "frm", None),
            P("frm"),
            P("src"),
        ),
        out_specs=(P("src", "frm", None), P(None, "frm")),
        check_vma=False,
    )
```

```python
import math

import jax
import jax.numpy as jnp
import numpy as np
from jax import lax
from jax.experimental import pallas as pl
from jax.experimental.pallas import tpu as pltpu
from jax.sharding import PartitionSpec as P

K = 64
GROUP = 2048
ITERS = 3
LANES = 128
BLOCK = 512
SPLIT = False

step_size = 0.5
shrink_one = 0.05
group_weight = 0.03
epsilon = 1e-06

F32 = jnp.float32
BF16 = jnp.bfloat16
HIGHEST = lax.Precision.HIGHEST
PARAMS = pltpu.CompilerParams(vmem_limit_bytes=16 * 1024 * 1024)


def windowed_cosines():
    t = np.arange(K)[:, None] + 0.5
    k = np.arange(K)[None, :] + 0.5
    return (np.sin(np.pi * t / K) * np.sqrt(2.0 / K) * np.cos(np.pi * k * t / K)).astype(np.float32)


def split(x):
    high = x.astype(BF16)
    return high, (x - high.astype(F32)).astype(BF16)


def dot(a, b):
    return jnp.dot(a, b, preferred_element_type=F32)


def dot_t(a, b):
    return lax.dot_general(a, b, (((1,), (1,)), ((), ())), preferred_element_type=F32)


def to_samples(atoms_ref, sums):
    high, low = split(sums)
    return dot(atoms_ref[0], high) + dot(atoms_ref[0], low) + dot(atoms_ref[1], high)


def group_scale(power, tau):
    return jnp.maximum(0.0, 1.0 - tau / jnp.sqrt(power + epsilon))


def first_kernel(
    where_ref, offsets_hbm, wave_hbm, group_hbm, depth_hbm, measured_hbm, coef_hbm, lead_hbm,
    table_ref, table_t_ref, mine_ref, theirs_ref, marks_ref, rows_ref, depth_ref, coef_ref, lead_ref,
    offsets_ref, wave_ref, group_ref, measured_ref, acc_ref, coef_sem, lead_sem, small_sem,
):
    total = table_ref.shape[2]
    own = mine_ref.shape[0]
    sources = lead_ref.shape[1]
    blocks = lead_sem.shape[0]
    block = sources // blocks
    pairs = (
        (offsets_hbm, offsets_ref), (wave_hbm, wave_ref), (group_hbm, group_ref), (measured_hbm, measured_ref),
        (depth_hbm, depth_ref),
    )
    small = [pltpu.make_async_copy(a, b, small_sem.at[n]) for n, (a, b) in enumerate(pairs)]
    for load in small:
        load.start()
    loads = []
    for j in range(blocks):
        cols = slice(j * block, (j + 1) * block)
        loads.append(
            (
                pltpu.make_async_copy(lead_hbm.at[:, cols], lead_ref.at[:, cols], lead_sem.at[j]),
                pltpu.make_async_copy(coef_hbm.at[:, cols], coef_ref.at[:, cols], coef_sem.at[j]),
            )
        )
        for load in loads[-1]:
            load.start()
    for load in small:
        load.wait()

    groups = group_ref[...]
    marks_ref[0] = jnp.sum((groups == groups[0:1, 0:1]).astype(jnp.int32))
    marks_ref[1] = where_ref[1]
    for t in range(rows_ref.shape[0]):
        rows_ref[t] = measured_ref[t * LANES : (t + 1) * LANES, :].T
    wave = wave_ref[...]
    order = lax.broadcasted_iota(jnp.int32, (total, K), 0)
    sample = (order + where_ref[0]) % total
    position = lax.broadcasted_iota(jnp.int32, (total, K), 1)
    for f in range(offsets_ref.shape[0]):
        delay = (sample - offsets_ref[f] + total) % total
        placing = (delay == position).astype(F32)
        part_t = jnp.dot(placing, wave, precision=HIGHEST, preferred_element_type=F32)
        rows = slice(f * K, (f + 1) * K)
        table_t_ref[0, :, rows], table_t_ref[1, :, rows] = split(part_t)
        table_ref[0, rows, :], table_ref[1, rows, :] = split(part_t.T)

    for j in range(blocks):
        for load in loads[j]:
            load.wait()
        cols = slice(j * block, (j + 1) * block)
        part = dot_t((coef_ref[:, cols] * depth_ref[:, cols]).astype(BF16), lead_ref[:, cols])
        if j == 0:
            acc_ref[...] = part
        else:
            acc_ref[...] += part
    samples = to_samples(table_t_ref, acc_ref[...])
    mine_ref[...] = samples[:own]
    theirs_ref[...] = samples[own:].astype(BF16)


def step_kernel(
    marks_ref, own_ref, other_ref, table_ref, table_t_ref, depth_ref, state_ref, lead_ref,
    *rest, width, predict, first, block,
):
    if not first:
        scale_ref, *rest = rest
    new_ref, power_ref, *rest = rest
    if predict:
        mine_ref, theirs_ref, rows_ref, samples_ref, turned_ref, weighted_ref = rest
    else:
        rows_ref, samples_ref, turned_ref = rest
    coefs, sources = state_ref.shape
    tiles = lead_ref.shape[0] // LANES
    own = table_ref.shape[2] // 2

    for h, ref in enumerate((own_ref, other_ref)):
        rows_ref[h] = ref[...].astype(F32)
        for t in range(tiles):
            lanes = slice(t * LANES, (t + 1) * LANES)
            part = rows_ref[h, pl.ds(t, own, stride=width), :]
            samples_ref[h * own : (h + 1) * own, lanes] = part.astype(BF16)
    turned = dot(table_ref[0], samples_ref[...]) + dot(table_ref[1], samples_ref[...])
    if SPLIT:
        turned_ref[:coefs], turned_ref[coefs:] = split(turned)
    else:
        turned_ref[...] = turned.astype(BF16)

    start = marks_ref[0]
    bounds = (start, start + GROUP)
    scales = None if first else [scale_ref[g : g + 1, 0:1] for g in range(3)]
    sums = [jnp.zeros((1, block), F32) for _ in range(4)]
    for j in range(sources // block):
        cols = slice(j * block, (j + 1) * block)
        half = j * block // GROUP
        gradient = dot(turned_ref[...], lead_ref[:, cols])
        if SPLIT:
            gradient = gradient[:coefs] + gradient[coefs:]
        source = j * block + lax.broadcasted_iota(jnp.int32, (1, block), 1)
        before = source < bounds[half]
        depth = depth_ref[:, cols]
        state = state_ref[:, cols]
        if not first:
            state = state * jnp.where(before, scales[half], scales[half + 1])
        moved = state + (step_size * depth) * gradient
        shrunk = moved - jnp.clip(moved, -shrink_one, shrink_one)
        new_ref[:, cols] = shrunk
        if predict:
            weighted = (shrunk * depth).astype(BF16)
            inner = slice(j * block - half * GROUP, (j + 1) * block - half * GROUP)
            none = jnp.zeros((), BF16)
            weighted_ref[half, :coefs, inner] = jnp.where(before, weighted, none)
            weighted_ref[half, coefs:, inner] = jnp.where(before, none, weighted)
        squares = jnp.sum(shrunk * shrunk, axis=0, keepdims=True)
        sums[2 * half] += jnp.where(before, squares, 0.0)
        sums[2 * half + 1] += jnp.where(before, 0.0, squares)
    power_ref[...] = jnp.zeros_like(power_ref)
    for g, total in enumerate((sums[0], sums[1] + sums[2], sums[3])):
        power_ref[g : g + 1, :] = jnp.broadcast_to(jnp.sum(total, axis=1, keepdims=True), (1, LANES))

    if predict:
        halves = [dot_t(weighted_ref[h], lead_ref[:, h * GROUP : (h + 1) * GROUP]) for h in range(2)]
        parts = (halves[0][:coefs], halves[0][coefs:] + halves[1][:coefs], halves[1][coefs:])
        for g in range(3):
            samples = to_samples(table_t_ref, parts[g])
            mine_ref[g * own : (g + 1) * own, :] = samples[:own]
            theirs_ref[g * own : (g + 1) * own, :] = samples[own:].astype(BF16)
        high, low = split(power_ref[...])
        for t in range(tiles):
            lanes = slice(t * LANES, (t + 1) * LANES)
            theirs_ref[3 * own : 3 * own + 16, lanes] = jnp.concatenate([high, low], axis=0)


def first_fold_kernel(mine_ref, theirs_ref, out_ref, rows_ref):
    own = mine_ref.shape[0]
    tiles = mine_ref.shape[1] // LANES
    for t in range(tiles):
        lanes = slice(t * LANES, (t + 1) * LANES)
        rows_ref[pl.ds(t, own, stride=tiles), :] = mine_ref[:, lanes] + theirs_ref[:, lanes].astype(F32)
    out_ref[...] = rows_ref[...].astype(BF16)


def fold_kernel(mine_ref, theirs_ref, power_ref, out_ref, chip_ref, rows_ref, *, tau):
    own = mine_ref.shape[0] // 3
    tiles = mine_ref.shape[1] // LANES
    theirs = theirs_ref[3 * own : 3 * own + 16, :LANES].astype(F32)
    chip = power_ref[...] + theirs[:8] + theirs[8:]
    chip_ref[...] = chip
    middle = group_scale(chip[1:2, :], tau)
    for g, part in enumerate((1, 0, 2)):
        for t in range(tiles):
            lanes = slice(t * LANES, (t + 1) * LANES)
            rows = slice(part * own, (part + 1) * own)
            total = mine_ref[rows, lanes] + theirs_ref[rows, lanes].astype(F32)
            if part == 1:
                total = total * middle
            rows_ref[pl.ds(g * tiles + t, own, stride=16), :] = total
    for g, part in enumerate((0, 2)):
        value = chip[part : part + 1, :]
        high = value.astype(BF16).astype(F32)
        for n, term in enumerate((high, value - high)):
            at = 3 * tiles + 2 * g + n
            rows_ref[pl.ds(at, own, stride=16), :] = jnp.broadcast_to(term, (own, LANES))
    out_ref[...] = rows_ref[...].astype(BF16)


def send_residual(row, out_ref, rows_ref, tiles, last):
    own = out_ref.shape[0] // (2 * tiles if last else tiles)
    if last:
        high = row.astype(BF16).astype(F32)
        row = jnp.concatenate([high, row - high], axis=0)
    out_ref[...] = jnp.concatenate([row.astype(BF16)] * own, axis=0)


def first_owner_kernel(marks_ref, got_ref, measured_ref, out_ref, rows_ref):
    me = marks_ref[1]
    tiles = measured_ref.shape[0]
    senders = got_ref.shape[0] // tiles
    rows_ref[...] = got_ref[...].astype(F32)
    row = [
        measured_ref[t, pl.ds(me, 1), :]
        - jnp.sum(rows_ref[pl.ds(t, senders, stride=tiles), :], axis=0, keepdims=True)
        for t in range(tiles)
    ]
    send_residual(jnp.concatenate(row, axis=0), out_ref, rows_ref, tiles, False)


def owner_kernel(marks_ref, got_ref, measured_ref, chip_ref, out_ref, scale_ref, rows_ref, edges_ref, *, tau, last):
    me = marks_ref[1]
    tiles = measured_ref.shape[0]
    senders = got_ref.shape[0] // 16
    rows_ref[...] = got_ref[...].astype(F32)

    def of(k):
        return rows_ref[pl.ds(k, senders, stride=16), :]

    front = of(3 * tiles) + of(3 * tiles + 1)
    back = of(3 * tiles + 2) + of(3 * tiles + 3)
    before = jnp.concatenate([back[senders - 1 :], back[: senders - 1]], axis=0)
    front_scale = group_scale(front + before, tau)
    back_scale = jnp.concatenate([front_scale[1:], front_scale[:1]], axis=0)
    row = []
    for t in range(tiles):
        parts = of(t) + front_scale * of(tiles + t) + back_scale * of(2 * tiles + t)
        row.append(measured_ref[t, pl.ds(me, 1), :] - jnp.sum(parts, axis=0, keepdims=True))
    send_residual(jnp.concatenate(row, axis=0), out_ref, rows_ref, tiles, last)
    edges_ref[0] = front_scale
    edges_ref[1] = back_scale
    scale_ref[...] = jnp.zeros_like(scale_ref)
    scale_ref[0:1, :] = edges_ref[0, pl.ds(me, 1), :]
    scale_ref[1:2, :] = group_scale(chip_ref[1:2, :], tau)
    scale_ref[2:3, :] = edges_ref[1, pl.ds(me, 1), :]


def add_kernel(a_ref, b_ref, out_ref):
    out_ref[...] = a_ref[...] + b_ref[...]


def residual_kernel(own_ref, out_ref, rows_ref):
    own = out_ref.shape[1]
    tiles = out_ref.shape[0] // LANES
    rows_ref[...] = own_ref[...].astype(F32)
    for t in range(tiles):
        high = rows_ref[pl.ds(t, own, stride=2 * tiles), :]
        low = rows_ref[pl.ds(tiles + t, own, stride=2 * tiles), :]
        out_ref[t * LANES : (t + 1) * LANES, :] = (high + low).T


def last_kernel(marks_ref, state_ref, chip_ref, before_ref, after_ref, out_hbm, scaled_ref, sem, *, tau):
    blocks, _, block = scaled_ref.shape
    first = group_scale(chip_ref[0:1, 0:1] + before_ref[2:3, 0:1], tau)
    middle = group_scale(chip_ref[1:2, 0:1], tau)
    last = group_scale(chip_ref[2:3, 0:1] + after_ref[0:1, 0:1], tau)
    start = marks_ref[0]
    stores = []
    for j in range(blocks):
        cols = slice(j * block, (j + 1) * block)
        source = j * block + lax.broadcasted_iota(jnp.int32, (1, block), 1)
        scale = jnp.where(source < start, first, jnp.where(source < start + GROUP, middle, last))
        scaled_ref[j] = state_ref[:, cols] * scale
        stores.append(pltpu.make_async_copy(scaled_ref.at[j], out_hbm.at[:, cols], sem.at[j]))
        stores[-1].start()
    for store in stores:
        store.wait()


SMEM = pl.BlockSpec(memory_space=pltpu.SMEM)
VMEM = pl.BlockSpec(memory_space=pltpu.VMEM)
HBM = pl.BlockSpec(memory_space=pltpu.HBM)


def struct(dtype, *shape):
    return jax.ShapeDtypeStruct(shape, dtype)


def call(kernel, name, ins, outs, out_specs=None, scratch=()):
    return pl.pallas_call(
        kernel, in_specs=ins, out_specs=out_specs or [VMEM] * len(outs), out_shape=outs,
        scratch_shapes=list(scratch), compiler_params=PARAMS, name=name,
    )


def stay(x):
    return pltpu.with_memory_space_constraint(x, pltpu.HBM)


def first_call(where, offsets, groups, depth, measured, state, lead):
    coefs, sources = state.shape
    sensors, own = measured.shape
    total = 2 * own
    dma = pltpu.SemaphoreType.DMA((sources // BLOCK,))
    inputs = (offsets, jnp.asarray(windowed_cosines()), groups, depth, measured, state, lead)
    return call(
        first_kernel,
        "first_forward",
        [SMEM] + [HBM] * len(inputs),
        [
            struct(BF16, 2, coefs, total),
            struct(BF16, 2, total, coefs),
            struct(F32, own, sensors),
            struct(BF16, own, sensors),
            struct(jnp.int32, 2),
            struct(F32, sensors // LANES, own, LANES),
            struct(F32, 1, sources),
            struct(F32, coefs, sources),
            struct(BF16, sensors, sources),
        ],
        [VMEM, VMEM, VMEM, VMEM, SMEM, VMEM, VMEM, VMEM, VMEM],
        [
            pltpu.SMEM(offsets.shape, jnp.int32),
            pltpu.VMEM((K, K), F32),
            pltpu.VMEM((1, sources), jnp.int32),
            pltpu.VMEM((sensors, own), F32),
            pltpu.VMEM((coefs, sensors), F32),
            dma,
            dma,
            pltpu.SemaphoreType.DMA((5,)),
        ],
    )(where, *(stay(x) for x in inputs))


def step_call(marks, mine, others, table, table_t, scale, depth, state, lead, *, first, last):
    coefs, sources = state.shape
    sensors = lead.shape[0]
    own = table.shape[2] // 2
    tiles = sensors // LANES
    width = mine.shape[0] // own
    outs = [struct(F32, coefs, sources), struct(F32, 8, LANES)]
    scratch = [
        pltpu.VMEM((2, own * width, LANES), F32),
        pltpu.VMEM((2 * own, sensors), BF16),
        pltpu.VMEM(((2 if SPLIT else 1) * coefs, sensors), BF16),
    ]
    if not last:
        outs += [struct(F32, 3 * own, sensors), struct(BF16, 3 * own + 16, sensors)]
        scratch += [pltpu.VMEM((2, 2 * coefs, GROUP), BF16)]

    def kernel(*refs):
        step_kernel(*refs, width=width, predict=not last, first=first, block=BLOCK)

    ins = [marks, mine, others, table, table_t, depth, state, lead] + ([] if first else [scale])
    return call(kernel, "step", [SMEM] + [VMEM] * (len(ins) - 1), outs, None, scratch)(*ins)


def last_call(marks, state, chip, before, after, tau):
    coefs, sources = state.shape
    blocks = sources // BLOCK
    return call(
        lambda *refs: last_kernel(*refs, tau=tau),
        "scaled_estimate",
        [SMEM] + [VMEM] * 4,
        [struct(F32, coefs, sources)],
        [HBM],
        [pltpu.VMEM((blocks, coefs, BLOCK), F32), pltpu.SemaphoreType.DMA((blocks,))],
    )(marks, state, chip, before, after)[0]


def shards(measured, lead_field, depth, coefficients, offsets, group_ids):
    sensors, own = measured.shape
    sources = lead_field.shape[1]
    frames = coefficients.shape[1]
    src_count, frm_count = lax.axis_size("src"), lax.axis_size("frm")
    coefs = frames * K
    tau = group_weight * math.sqrt(GROUP * frames * frm_count * K)
    tiles = sensors // LANES
    across = [(i, (i + 1) % frm_count) for i in range(frm_count)]
    ahead = [(i, (i + 1) % src_count) for i in range(src_count)]
    behind = [((i + 1) % src_count, i) for i in range(src_count)]

    where = jnp.stack([lax.axis_index("frm") * own, lax.axis_index("src")])

    def exchange(rows):
        return lax.all_to_all(rows, "src", 0, 0, tiled=True)

    state = coefficients.transpose(1, 2, 0).reshape(coefs, sources)
    table, table_t, mine, theirs, marks, rows, depth_row, state, lead = first_call(
        where, offsets, group_ids.reshape(1, sources), depth.reshape(1, sources), measured, state, lead_field
    )
    folded = call(
        first_fold_kernel,
        "first_fold",
        [VMEM, VMEM],
        [struct(BF16, own * tiles, LANES)],
        None,
        [pltpu.VMEM((own * tiles, LANES), F32)],
    )(mine, lax.ppermute(theirs, "frm", across))[0]
    scale = None
    for iteration in range(ITERS):
        first, last = iteration == 0, iteration == ITERS - 1
        got = exchange(folded)
        width = 2 * tiles if last else tiles
        if first:
            row = call(
                first_owner_kernel,
                "first_owner",
                [SMEM, VMEM, VMEM],
                [struct(BF16, own * width, LANES)],
                None,
                [pltpu.VMEM((src_count * tiles, LANES), F32)],
            )(marks, got, rows)[0]
        else:
            row, scale = call(
                lambda *refs, last=last: owner_kernel(*refs, tau=tau, last=last),
                "owner",
                [SMEM, VMEM, VMEM, VMEM],
                [struct(BF16, own * width, LANES), struct(F32, 8, LANES)],
                None,
                [pltpu.VMEM((src_count * 16, LANES), F32), pltpu.VMEM((2, src_count, LANES), F32)],
            )(marks, got, rows, chip)
        mine = exchange(row)
        others = lax.ppermute(mine, "frm", across)
        results = step_call(
            marks, mine, others, table, table_t, scale, depth_row, state, lead, first=first, last=last
        )
        state, power = results[:2]
        if last:
            break
        folded, chip = call(
            lambda *refs: fold_kernel(*refs, tau=tau),
            "fold",
            [VMEM, VMEM, VMEM],
            [struct(BF16, own * 16, LANES), struct(F32, 8, LANES)],
            None,
            [pltpu.VMEM((own * 16, LANES), F32)],
        )(results[2], lax.ppermute(results[3], "frm", across), power)

    chip = call(add_kernel, "chip_power", [VMEM, VMEM], [struct(F32, 8, LANES)])(
        power, lax.ppermute(power, "frm", across)
    )[0]
    before = lax.ppermute(chip, "src", ahead)
    after = lax.ppermute(chip, "src", behind)
    residual = call(
        residual_kernel,
        "residual",
        [VMEM],
        [struct(F32, sensors, own)],
        None,
        [pltpu.VMEM((own * 2 * tiles, LANES), F32)],
    )(mine)[0]
    estimate = last_call(marks, state, chip, before, after, tau)
    return (estimate.reshape(frames, K, sources).transpose(2, 0, 1), residual)


def solution(mesh):
    return jax.shard_map(
        shards,
        mesh=mesh,
        in_specs=(
            P(None, "frm"),
            P(None, "src"),
            P("src"),
            P("src", "frm", None),
            P("frm"),
            P("src"),
        ),
        out_specs=(P("src", "frm", None), P(None, "frm")),
        check_vma=False,
    )
```

```python
import math

import jax
import jax.numpy as jnp
import numpy as np
from jax import lax
from jax.experimental import pallas as pl
from jax.experimental.pallas import tpu as pltpu
from jax.sharding import Mesh
from jax.sharding import PartitionSpec as P

K = 64
GROUP = 2048
ITERS = 3
LANES = 128
BLOCK = 512
SPILL = 64

step_size = 0.5
shrink_one = 0.05
group_weight = 0.03
epsilon = 1e-06

F32 = jnp.float32
BF16 = jnp.bfloat16
HIGHEST = lax.Precision.HIGHEST
PARAMS = pltpu.CompilerParams(vmem_limit_bytes=16 * 1024 * 1024)
AXES = {"x": 4, "z": 8, "y": 4}
SRC = ("x", "z", "y")
PLANE = ("x", "y")


def windowed_cosines():
    t = np.arange(K)[:, None] + 0.5
    k = np.arange(K)[None, :] + 0.5
    return (np.sin(np.pi * t / K) * np.sqrt(2.0 / K) * np.cos(np.pi * k * t / K)).astype(np.float32)


def split(x):
    high = x.astype(BF16)
    return high, (x - high.astype(F32)).astype(BF16)


def dot(a, b):
    return jnp.dot(a, b, preferred_element_type=F32)


def dot_t(a, b):
    return lax.dot_general(a, b, (((1,), (1,)), ((), ())), preferred_element_type=F32)


def to_samples(atoms_ref, sums):
    high, low = split(sums)
    return dot(atoms_ref[0], high) + dot(atoms_ref[0], low) + dot(atoms_ref[1], high)


def group_scale(power, tau):
    return jnp.maximum(0.0, 1.0 - tau / jnp.sqrt(power + epsilon))


def scales_of(chip_ref, before_ref, after_ref, tau):
    return (
        group_scale(chip_ref[0:1, :] + before_ref[2:3, :], tau),
        group_scale(chip_ref[1:2, :], tau),
        group_scale(chip_ref[2:3, :] + after_ref[0:1, :], tau),
    )


def first_kernel(
    where_ref, offsets_hbm, wave_hbm, group_hbm, depth_hbm, measured_hbm, coef_hbm, lead_hbm,
    table_ref, table_t_ref, mine_ref, theirs_ref, marks_ref, rows_ref, depth_ref, coef_ref, lead_ref,
    offsets_ref, wave_ref, group_ref, measured_ref, acc_ref, coef_sem, lead_sem, small_sem,
):
    total = table_ref.shape[2]
    own = mine_ref.shape[0]
    sources = lead_ref.shape[1]
    blocks = lead_sem.shape[0]
    block = sources // blocks
    pairs = (
        (offsets_hbm, offsets_ref), (wave_hbm, wave_ref), (group_hbm, group_ref), (measured_hbm, measured_ref),
        (depth_hbm, depth_ref),
    )
    small = [pltpu.make_async_copy(a, b, small_sem.at[n]) for n, (a, b) in enumerate(pairs)]
    for load in small:
        load.start()
    loads = []
    for j in range(blocks):
        cols = slice(j * block, (j + 1) * block)
        loads.append(
            (
                pltpu.make_async_copy(lead_hbm.at[:, cols], lead_ref.at[:, cols], lead_sem.at[j]),
                pltpu.make_async_copy(coef_hbm.at[:, cols], coef_ref.at[:, cols], coef_sem.at[j]),
            )
        )
        for load in loads[-1]:
            load.start()
    for load in small:
        load.wait()

    groups = group_ref[...]
    marks_ref[0] = jnp.sum((groups == groups[0:1, 0:1]).astype(jnp.int32))
    marks_ref[1] = where_ref[1]
    for t in range(measured_ref.shape[0] // LANES):
        lanes = slice(t * LANES, (t + 1) * LANES)
        rows_ref[:, lanes] = measured_ref[lanes, :].T
    wave = wave_ref[...]
    order = lax.broadcasted_iota(jnp.int32, (total, K), 0)
    sample = lax.rem(order + where_ref[0], total)
    position = lax.broadcasted_iota(jnp.int32, (total, K), 1)
    for f in range(offsets_ref.shape[0]):
        delay = lax.rem(sample - offsets_ref[f] + total, total)
        placing = (delay == position).astype(F32)
        part_t = jnp.dot(placing, wave, precision=HIGHEST, preferred_element_type=F32)
        rows = slice(f * K, (f + 1) * K)
        table_t_ref[0, :, rows], table_t_ref[1, :, rows] = split(part_t)
        table_ref[0, rows, :], table_ref[1, rows, :] = split(part_t.T)

    for j in range(blocks):
        for load in loads[j]:
            load.wait()
        cols = slice(j * block, (j + 1) * block)
        part = dot_t((coef_ref[:, cols] * depth_ref[:, cols]).astype(BF16), lead_ref[:, cols])
        if j == 0:
            acc_ref[...] = part
        else:
            acc_ref[...] += part
    samples = to_samples(table_t_ref, acc_ref[...])
    mine_ref[...] = samples[:own]
    theirs_ref[...] = samples[own : own + SPILL].astype(BF16)


def slabs(x):
    return [x[i : i + 8] for i in range(0, x.shape[0], 8)]


def step_kernel(
    marks_ref, own_ref, other_ref, table_ref, depth_ref, state_ref, lead_ref, *rest, first, last, block
):
    if not first:
        scale_ref, *rest = rest
    new_ref, power_ref, samples_ref, turned_ref = rest
    sources = state_ref.shape[1]
    own = table_ref.shape[2] // 2

    for h, ref in enumerate((own_ref, other_ref)):
        samples = ref[...]
        if last:
            samples = jnp.concatenate(slabs(samples.astype(F32))[::2], axis=0).astype(BF16)
        samples_ref[h * own : (h + 1) * own, :] = samples
    turned = dot(table_ref[0], samples_ref[...]) + dot(table_ref[1], samples_ref[...])
    turned_ref[...] = turned.astype(BF16)

    start = marks_ref[0]
    bounds = (start, start + GROUP)
    scales = None if first else [scale_ref[g : g + 1, 0:1] for g in range(3)]
    sums = [jnp.zeros((1, block), F32) for _ in range(4)]
    for j in range(sources // block):
        cols = slice(j * block, (j + 1) * block)
        half = j * block // GROUP
        gradient = dot(turned_ref[...], lead_ref[:, cols])
        source = j * block + lax.broadcasted_iota(jnp.int32, (1, block), 1)
        before = source < bounds[half]
        state = state_ref[:, cols]
        if not first:
            state = state * jnp.where(before, scales[half], scales[half + 1])
        moved = state + (step_size * depth_ref[:, cols]) * gradient
        shrunk = moved - jnp.clip(moved, -shrink_one, shrink_one)
        new_ref[:, cols] = shrunk
        squares = jnp.sum(shrunk * shrunk, axis=0, keepdims=True)
        sums[2 * half] += jnp.where(before, squares, 0.0)
        sums[2 * half + 1] += jnp.where(before, 0.0, squares)
    power_ref[...] = jnp.zeros_like(power_ref)
    for g, total in enumerate((sums[0], sums[1] + sums[2], sums[3])):
        power_ref[g : g + 1, :] = jnp.broadcast_to(jnp.sum(total, axis=1, keepdims=True), (1, LANES))


def forward_kernel(
    marks_ref, state_ref, depth_ref, lead_ref, table_t_ref, chip_ref, mine_ref, theirs_ref, weighted_ref, *,
    block, tau,
):
    coefs, sources = state_ref.shape
    own = mine_ref.shape[0] // 3
    start = marks_ref[0]
    bounds = (start, start + GROUP)
    none = jnp.zeros((), BF16)
    for j in range(sources // block):
        cols = slice(j * block, (j + 1) * block)
        half = j * block // GROUP
        before = j * block + lax.broadcasted_iota(jnp.int32, (1, block), 1) < bounds[half]
        weighted = (state_ref[:, cols] * depth_ref[:, cols]).astype(BF16)
        inner = slice(j * block - half * GROUP, (j + 1) * block - half * GROUP)
        weighted_ref[half, :coefs, inner] = jnp.where(before, weighted, none)
        weighted_ref[half, coefs:, inner] = jnp.where(before, none, weighted)
    halves = [dot_t(weighted_ref[h], lead_ref[:, h * GROUP : (h + 1) * GROUP]) for h in range(2)]
    middle = group_scale(chip_ref[1:2, 0:1], tau) * (halves[0][coefs:] + halves[1][:coefs])
    parts = (halves[0][:coefs], middle, halves[1][coefs:])
    for g in range(3):
        samples = to_samples(table_t_ref, parts[g])
        mine_ref[g * own : (g + 1) * own, :] = samples[:own]
        theirs_ref[g * SPILL : (g + 1) * SPILL, :] = samples[own : own + SPILL].astype(BF16)


def fold_kernel(mine_ref, theirs_ref, *rest, tau=None):
    *powers, out_ref = rest if tau is None else rest[:-1]
    own = out_ref.shape[0]
    if tau is None:
        mine, theirs = mine_ref[...], theirs_ref[...].astype(F32)
    else:
        scale_ref = rest[-1]
        scales = scales_of(*powers, tau)
        scale_ref[...] = jnp.zeros_like(scale_ref)
        mine, theirs = 0.0, 0.0
        for g, scale in enumerate(scales):
            scale_ref[g : g + 1, :] = scale
            scale = 1.0 if g == 1 else scale[:, 0:1]
            mine += scale * mine_ref[g * own : (g + 1) * own, :]
            theirs += scale * theirs_ref[g * SPILL : (g + 1) * SPILL, :].astype(F32)
    out_ref[:SPILL] = (mine[:SPILL] + theirs).astype(BF16)
    out_ref[SPILL:] = mine[SPILL:].astype(BF16)


def plane_kernel(got_ref, out_ref):
    total = sum(slabs(got_ref[...].astype(F32)))
    out_ref[...] = jnp.concatenate([total] * (out_ref.shape[0] // 8), axis=0)


def owner_kernel(marks_ref, got_ref, measured_ref, out_ref, *, last):
    at = pl.ds(pl.multiple_of(marks_ref[1] * 8, 8), 8)
    row = measured_ref[at, :] - sum(slabs(got_ref[...]))
    if last:
        high = row.astype(BF16).astype(F32)
        row = jnp.concatenate([high, row - high], axis=0)
    out_ref[...] = jnp.concatenate([row] * (out_ref.shape[0] // row.shape[0]), axis=0).astype(BF16)


def add_kernel(a_ref, b_ref, out_ref):
    out_ref[...] = a_ref[...] + b_ref[...]


def residual_kernel(own_ref, out_ref):
    pieces = slabs(own_ref[...].astype(F32))
    rows = jnp.concatenate([high + low for high, low in zip(pieces[::2], pieces[1::2])], axis=0)
    for t in range(out_ref.shape[0] // LANES):
        lanes = slice(t * LANES, (t + 1) * LANES)
        out_ref[lanes, :] = rows[:, lanes].T


def last_kernel(marks_ref, state_ref, chip_ref, before_ref, after_ref, out_hbm, scaled_ref, sem, *, tau):
    blocks, _, block = scaled_ref.shape
    scales = [scale[:, 0:1] for scale in scales_of(chip_ref, before_ref, after_ref, tau)]
    start = marks_ref[0]
    bounds = (start, start + GROUP)
    stores = []
    for j in range(blocks):
        cols = slice(j * block, (j + 1) * block)
        half = j * block // GROUP
        before = j * block + lax.broadcasted_iota(jnp.int32, (1, block), 1) < bounds[half]
        scaled_ref[j] = state_ref[:, cols] * jnp.where(before, scales[half], scales[half + 1])
        stores.append(pltpu.make_async_copy(scaled_ref.at[j], out_hbm.at[:, cols], sem.at[j]))
        stores[-1].start()
    for store in stores:
        store.wait()


SMEM = pl.BlockSpec(memory_space=pltpu.SMEM)
VMEM = pl.BlockSpec(memory_space=pltpu.VMEM)
HBM = pl.BlockSpec(memory_space=pltpu.HBM)


def struct(dtype, *shape):
    return jax.ShapeDtypeStruct(shape, dtype)


def call(kernel, name, args, outs, *, ins=None, out_specs=None, scratch=(), cost=None):
    return pl.pallas_call(
        kernel, in_specs=ins or [VMEM] * len(args), out_specs=out_specs or [VMEM] * len(outs), out_shape=outs,
        scratch_shapes=list(scratch), compiler_params=PARAMS, name=name, cost_estimate=cost,
    )(*args)


def stay(x):
    return pltpu.with_memory_space_constraint(x, pltpu.HBM)


def first_call(where, offsets, groups, depth, measured, state, lead):
    coefs, sources = state.shape
    sensors, own = measured.shape
    total = 2 * own
    dma = pltpu.SemaphoreType.DMA((sources // BLOCK,))
    inputs = (offsets, jnp.asarray(windowed_cosines()), groups, depth, measured, state, lead)
    return call(
        first_kernel,
        "first_forward",
        [where] + [stay(x) for x in inputs],
        [
            struct(BF16, 2, coefs, total),
            struct(BF16, 2, total, coefs),
            struct(F32, own, sensors),
            struct(BF16, SPILL, sensors),
            struct(jnp.int32, 2),
            struct(F32, own, sensors),
            struct(F32, 1, sources),
            struct(F32, coefs, sources),
            struct(BF16, sensors, sources),
        ],
        ins=[SMEM] + [HBM] * len(inputs),
        out_specs=[VMEM, VMEM, VMEM, VMEM, SMEM, VMEM, VMEM, VMEM, VMEM],
        scratch=[
            pltpu.SMEM(offsets.shape, jnp.int32),
            pltpu.VMEM((K, K), F32),
            pltpu.VMEM((1, sources), jnp.int32),
            pltpu.VMEM((sensors, own), F32),
            pltpu.VMEM((coefs, sensors), F32),
            dma,
            dma,
            pltpu.SemaphoreType.DMA((5,)),
        ],
    )


def step_call(marks, mine, others, table, scale, depth, state, lead, *, first, last):
    coefs, sources = state.shape
    sensors = lead.shape[0]
    args = [marks, mine, others, table, depth, state, lead] + ([] if first else [scale])
    return call(
        lambda *refs: step_kernel(*refs, first=first, last=last, block=BLOCK),
        "step",
        args,
        [struct(F32, coefs, sources), struct(F32, 8, LANES)],
        ins=[SMEM] + [VMEM] * (len(args) - 1),
        scratch=[pltpu.VMEM((table.shape[2], sensors), BF16), pltpu.VMEM((coefs, sensors), BF16)],
    )


def forward_call(marks, state, depth, lead, table_t, chip, tau):
    coefs, sources = state.shape
    sensors = lead.shape[0]
    own = table_t.shape[1] // 2
    return call(
        lambda *refs: forward_kernel(*refs, block=BLOCK, tau=tau),
        "forward",
        [marks, state, depth, lead, table_t, chip],
        [struct(F32, 3 * own, sensors), struct(BF16, 3 * SPILL, sensors)],
        ins=[SMEM] + [VMEM] * 5,
        scratch=[pltpu.VMEM((2, 2 * coefs, GROUP), BF16)],
        cost=pl.CostEstimate(flops=4 * coefs * sources * sensors, bytes_accessed=8 << 20, transcendentals=0),
    )


def last_call(marks, state, chip, before, after, tau):
    coefs, sources = state.shape
    blocks = sources // BLOCK
    return call(
        lambda *refs: last_kernel(*refs, tau=tau),
        "scaled_estimate",
        [marks, state, chip, before, after],
        [struct(F32, coefs, sources)],
        ins=[SMEM] + [VMEM] * 4,
        out_specs=[HBM],
        scratch=[pltpu.VMEM((blocks, coefs, BLOCK), F32), pltpu.SemaphoreType.DMA((blocks,))],
    )[0]


def shards(measured, lead_field, depth, coefficients, offsets, group_ids):
    sensors, own = measured.shape
    sources = lead_field.shape[1]
    frames = coefficients.shape[1]
    frm_count = lax.axis_size("frm")
    src_count = math.prod(AXES.values())
    coefs = frames * K
    tau = group_weight * math.sqrt(GROUP * frames * frm_count * K)
    across = [(i, (i + 1) % frm_count) for i in range(frm_count)]
    ahead = [(i, (i + 1) % src_count) for i in range(src_count)]
    behind = [((i + 1) % src_count, i) for i in range(src_count)]
    where = jnp.stack([lax.axis_index("frm") * own, lax.axis_index(PLANE)])

    def exchange(rows, axes):
        return lax.all_to_all(rows, axes, 0, 0, tiled=True)

    def chip_sums(power):
        chip = call(add_kernel, "chip_power", [power, lax.ppermute(power, "frm", across)], [struct(F32, 8, LANES)])[0]
        return chip, lax.ppermute(chip, SRC, ahead), lax.ppermute(chip, SRC, behind)

    state = coefficients.transpose(1, 2, 0).reshape(coefs, sources)
    table, table_t, mine, theirs, marks, rows, depth_row, state, lead = first_call(
        where, offsets, group_ids.reshape(1, sources), depth.reshape(1, sources), measured, state, lead_field
    )
    folded = call(
        fold_kernel, "first_fold", [mine, lax.ppermute(theirs, "frm", across)], [struct(BF16, own, sensors)]
    )[0]
    scale = None
    for iteration in range(ITERS):
        first, last = iteration == 0, iteration == ITERS - 1
        plane = call(
            plane_kernel, "plane_sum", [exchange(folded, PLANE)], [struct(F32, 8 * AXES["z"], sensors)]
        )[0]
        slab = call(
            lambda *refs, last=last: owner_kernel(*refs, last=last),
            "owner",
            [marks, exchange(plane, "z"), rows],
            [struct(BF16, own * (2 if last else 1), sensors)],
            ins=[SMEM, VMEM, VMEM],
        )[0]
        mine = exchange(slab, PLANE)
        others = lax.ppermute(mine, "frm", across)
        state, power = step_call(
            marks, mine, others, table, scale, depth_row, state, lead, first=first, last=last
        )
        chip, before, after = chip_sums(power)
        if not last:
            parts, theirs = forward_call(marks, state, depth_row, lead, table_t, chip, tau)
            theirs, before, after = lax.optimization_barrier((theirs, before, after))
            folded, scale = call(
                lambda *refs: fold_kernel(*refs, tau=tau),
                "fold",
                [parts, lax.ppermute(theirs, "frm", across), chip, before, after],
                [struct(BF16, own, sensors), struct(F32, 8, LANES)],
            )

    residual = call(residual_kernel, "residual", [mine], [struct(F32, sensors, own)])[0]
    estimate = last_call(marks, state, chip, before, after, tau)
    return (estimate.reshape(frames, K, sources).transpose(2, 0, 1), residual)


def solution(mesh):
    fine = Mesh(mesh.devices.reshape(*AXES.values(), mesh.shape["frm"]), (*AXES, "frm"))
    return jax.shard_map(
        shards,
        mesh=fine,
        in_specs=(
            P(None, "frm"),
            P(None, SRC),
            P(SRC),
            P(SRC, "frm", None),
            P("frm"),
            P(SRC),
        ),
        out_specs=(P(SRC, "frm", None), P(None, "frm")),
        check_vma=False,
    )
```

```python
import math

import jax
import jax.numpy as jnp
import ml_dtypes
import numpy as np
from jax import lax
from jax.experimental import pallas as pl
from jax.experimental.pallas import tpu as pltpu
from jax.sharding import Mesh
from jax.sharding import PartitionSpec as P

K = 64
GROUP = 2048
ITERS = 3
LANES = 128
BLOCK = 512
step_size = 0.5
shrink_one = 0.05
group_weight = 0.03
epsilon = 1e-06

F32 = jnp.float32
BF16 = jnp.bfloat16
HIGHEST = lax.Precision.HIGHEST
PARAMS = pltpu.CompilerParams(vmem_limit_bytes=16 * 1024 * 1024)
AXES = {"x": 4, "z": 8, "y": 4}
SRC = ("x", "z", "y")
PLANE = ("x", "y")
PLANES = ("frm", "x", "y")


def windowed_cosines():
    t = np.arange(K)[:, None] + 0.5
    k = np.arange(K)[None, :] + 0.5
    wave = np.sin(np.pi * t / K) * np.sqrt(2.0 / K) * np.cos(np.pi * k * t / K)
    high = wave.astype(ml_dtypes.bfloat16)
    low = (wave - high.astype(np.float64)).astype(ml_dtypes.bfloat16)
    return np.stack([high, low, high.T, low.T])


def split(x):
    high = x.astype(BF16)
    return high, (x - high.astype(F32)).astype(BF16)


def dot(a, b):
    return jnp.dot(a, b, preferred_element_type=F32)


def dot_t(a, b):
    return lax.dot_general(a, b, (((1,), (1,)), ((), ())), preferred_element_type=F32)


def to_samples(atoms_ref, sums):
    high, low = split(sums)
    return dot(atoms_ref[0], high) + dot(atoms_ref[0], low) + dot(atoms_ref[1], high)


def group_scale(power, tau):
    return jnp.maximum(0.0, 1.0 - tau / jnp.sqrt(power + epsilon))


def scales_of(powers, tau):
    mine, pair, before, before_pair, after, after_pair = (ref[...] for ref in powers)
    chip = mine + pair
    return (
        group_scale(chip[0:1] + (before + before_pair)[2:3], tau),
        group_scale(chip[1:2], tau),
        group_scale(chip[2:3] + (after + after_pair)[0:1], tau),
    )


def first_kernel(
    where_ref, offsets_hbm, wave_hbm, group_hbm, depth_hbm, measured_hbm, coef_hbm, lead_hbm,
    table_ref, table_t_ref, out_ref, marks_ref, rows_ref, depth_ref, coef_ref, lead_ref,
    offsets_ref, wave_ref, group_ref, measured_ref, acc_ref, coef_sem, lead_sem, small_sem,
):
    total = table_ref.shape[2]
    sources = lead_ref.shape[1]
    blocks = lead_sem.shape[0]
    block = sources // blocks
    pairs = (
        (offsets_hbm, offsets_ref), (wave_hbm, wave_ref), (group_hbm, group_ref), (measured_hbm, measured_ref),
        (depth_hbm, depth_ref),
    )
    small = [pltpu.make_async_copy(a, b, small_sem.at[n]) for n, (a, b) in enumerate(pairs)]
    for load in small:
        load.start()
    loads = []
    for j in range(blocks):
        cols = slice(j * block, (j + 1) * block)
        loads.append(
            (
                pltpu.make_async_copy(lead_hbm.at[:, cols], lead_ref.at[:, cols], lead_sem.at[j]),
                pltpu.make_async_copy(coef_hbm.at[:, cols], coef_ref.at[:, cols], coef_sem.at[j]),
            )
        )
        for load in loads[-1]:
            load.start()
    for load in small:
        load.wait()

    groups = group_ref[...]
    marks_ref[0] = jnp.sum((groups == groups[0:1, 0:1]).astype(jnp.int32))
    marks_ref[1] = where_ref[1]
    marks_ref[2] = where_ref[0]
    for t in range(measured_ref.shape[0] // LANES):
        lanes = slice(t * LANES, (t + 1) * LANES)
        rows_ref[:, lanes] = measured_ref[lanes, :].T
    for f in range(offsets_ref.shape[0]):
        rows = slice(f * K, (f + 1) * K)
        for axis in range(2):
            shape = (total, K) if axis == 0 else (K, total)
            sample = lax.broadcasted_iota(jnp.int32, shape, axis)
            position = lax.broadcasted_iota(jnp.int32, shape, 1 - axis)
            delay = lax.rem(sample - offsets_ref[f] + total, total)
            placing = (delay == position).astype(F32).astype(BF16)
            for h in range(2):
                if axis == 0:
                    table_t_ref[h, :, rows] = dot(placing, wave_ref[h]).astype(BF16)
                else:
                    table_ref[h, rows, :] = dot(wave_ref[2 + h], placing).astype(BF16)

    for j in range(blocks):
        for load in loads[j]:
            load.wait()
        cols = slice(j * block, (j + 1) * block)
        part = dot_t((coef_ref[:, cols] * depth_ref[:, cols]).astype(BF16), lead_ref[:, cols])
        if j == 0:
            acc_ref[...] = part
        else:
            acc_ref[...] += part
    out_ref[...] = to_samples(table_t_ref, acc_ref[...]).astype(BF16)


def slabs(x):
    return [x[i : i + 8] for i in range(0, x.shape[0], 8)]


def step_kernel(
    marks_ref, got_ref, *rest, first, last, block
):
    if last:
        other_ref, *rest = rest
    table_ref, depth_ref, state_ref, lead_ref, *rest = rest
    if not first:
        scale_ref, *rest = rest
    new_ref, power_ref, turned_ref, *rest = rest
    sources = state_ref.shape[1]
    if last:
        (samples_ref,) = rest
        own = samples_ref.shape[0] // 2
        for ref, core in ((got_ref, marks_ref[2]), (other_ref, 1 - marks_ref[2])):
            at = pl.ds(pl.multiple_of(core * own, own), own)
            samples_ref[at, :] = jnp.concatenate(slabs(ref[...].astype(F32))[::2], axis=0).astype(BF16)
    else:
        samples_ref = got_ref
    turned = dot(table_ref[0], samples_ref[...]) + dot(table_ref[1], samples_ref[...])
    turned_ref[...] = turned.astype(BF16)

    start = marks_ref[0]
    bounds = (start, start + GROUP)
    scales = None if first else [scale_ref[g : g + 1, 0:1] for g in range(3)]
    sums = [jnp.zeros((1, block), F32) for _ in range(4)]
    for j in range(sources // block):
        cols = slice(j * block, (j + 1) * block)
        half = j * block // GROUP
        gradient = dot(turned_ref[...], lead_ref[:, cols])
        source = j * block + lax.broadcasted_iota(jnp.int32, (1, block), 1)
        before = source < bounds[half]
        state = state_ref[:, cols]
        if not first:
            state = state * jnp.where(before, scales[half], scales[half + 1])
        moved = state + (step_size * depth_ref[:, cols]) * gradient
        shrunk = moved - jnp.clip(moved, -shrink_one, shrink_one)
        new_ref[:, cols] = shrunk
        squares = jnp.sum(shrunk * shrunk, axis=0, keepdims=True)
        sums[2 * half] += jnp.where(before, squares, 0.0)
        sums[2 * half + 1] += jnp.where(before, 0.0, squares)
    power_ref[...] = jnp.zeros_like(power_ref)
    for g, total in enumerate((sums[0], sums[1] + sums[2], sums[3])):
        power_ref[g : g + 1, :] = jnp.broadcast_to(jnp.sum(total, axis=1, keepdims=True), (1, LANES))


def forward_kernel(
    marks_ref, state_ref, depth_ref, lead_ref, table_t_ref, power_ref, pair_ref, out_ref, weighted_ref, *,
    block, tau,
):
    coefs, sources = state_ref.shape
    total = out_ref.shape[0] // 3
    start = marks_ref[0]
    bounds = (start, start + GROUP)
    none = jnp.zeros((), BF16)
    for j in range(sources // block):
        cols = slice(j * block, (j + 1) * block)
        half = j * block // GROUP
        before = j * block + lax.broadcasted_iota(jnp.int32, (1, block), 1) < bounds[half]
        weighted = (state_ref[:, cols] * depth_ref[:, cols]).astype(BF16)
        inner = slice(j * block - half * GROUP, (j + 1) * block - half * GROUP)
        weighted_ref[half, :coefs, inner] = jnp.where(before, weighted, none)
        weighted_ref[half, coefs:, inner] = jnp.where(before, none, weighted)
    halves = [dot_t(weighted_ref[h], lead_ref[:, h * GROUP : (h + 1) * GROUP]) for h in range(2)]
    middle = group_scale(power_ref[1:2, 0:1] + pair_ref[1:2, 0:1], tau) * (halves[0][coefs:] + halves[1][:coefs])
    parts = (halves[0][:coefs], middle, halves[1][coefs:])
    for g in range(3):
        out_ref[g * total : (g + 1) * total, :] = to_samples(table_t_ref, parts[g])


def fold_kernel(parts_ref, *rest, tau):
    *powers, out_ref, scale_ref = rest
    total = out_ref.shape[0]
    scale_ref[...] = jnp.zeros_like(scale_ref)
    scales = scales_of(powers, tau)
    for g, scale in enumerate(scales):
        scale_ref[g : g + 1, :] = scale
    first, middle, last = (parts_ref[g * total : (g + 1) * total, :] for g in range(3))
    out_ref[...] = (scales[0][:, 0:1] * first + middle + scales[2][:, 0:1] * last).astype(BF16)


def plane_kernel(got_ref, out_ref):
    total = sum(slabs(got_ref[...].astype(F32)))
    out_ref[...] = jnp.concatenate([total] * (out_ref.shape[0] // 8), axis=0)


def owner_kernel(marks_ref, got_ref, measured_ref, out_ref, *, last):
    at = pl.ds(pl.multiple_of(marks_ref[1] * 8, 8), 8)
    row = measured_ref[at, :] - sum(slabs(got_ref[...]))
    if last:
        high = row.astype(BF16).astype(F32)
        row = jnp.concatenate([high, row - high], axis=0)
    out_ref[...] = jnp.concatenate([row] * (out_ref.shape[0] // row.shape[0]), axis=0).astype(BF16)


def residual_kernel(own_ref, out_ref):
    pieces = slabs(own_ref[...].astype(F32))
    rows = jnp.concatenate([high + low for high, low in zip(pieces[::2], pieces[1::2])], axis=0)
    for t in range(out_ref.shape[0] // LANES):
        lanes = slice(t * LANES, (t + 1) * LANES)
        out_ref[lanes, :] = rows[:, lanes].T


def estimate_kernel(marks_ref, state_ref, *rest, tau, middle):
    if middle:
        power_ref, pair_ref, out_hbm, scaled_ref, sem = rest
        scales = [None, group_scale(power_ref[1:2, 0:1] + pair_ref[1:2, 0:1], tau), None]
    else:
        *powers, _, out_hbm, scaled_ref, sem = rest
        scales = [scale[:, 0:1] for scale in scales_of(powers, tau)]
    blocks, _, block = scaled_ref.shape
    start = marks_ref[0]
    bounds = (start, start + GROUP)
    wanted, stores = [], []
    for j in range(blocks):
        cols = slice(j * block, (j + 1) * block)
        half = j * block // GROUP
        inside = bounds[0] <= j * block if half == 0 else (j + 1) * block <= bounds[1]
        wanted.append(inside if middle else jnp.logical_not(inside))
        stores.append(pltpu.make_async_copy(scaled_ref.at[j], out_hbm.at[:, cols], sem.at[j]))

        @pl.when(wanted[j])
        def _():
            if middle:
                scale = scales[1]
            else:
                before = j * block + lax.broadcasted_iota(jnp.int32, (1, block), 1) < bounds[half]
                scale = jnp.where(before, scales[half], scales[half + 1])
            scaled_ref[j] = state_ref[:, cols] * scale
            stores[j].start()

    for j in range(blocks):
        pl.when(wanted[j])(stores[j].wait)


SMEM = pl.BlockSpec(memory_space=pltpu.SMEM)
VMEM = pl.BlockSpec(memory_space=pltpu.VMEM)
HBM = pl.BlockSpec(memory_space=pltpu.HBM)


def struct(dtype, *shape):
    return jax.ShapeDtypeStruct(shape, dtype)


def call(kernel, name, args, outs, *, ins=None, out_specs=None, scratch=(), cost=None, alias=None):
    return pl.pallas_call(
        kernel, in_specs=ins or [VMEM] * len(args), out_specs=out_specs or [VMEM] * len(outs), out_shape=outs,
        scratch_shapes=list(scratch), compiler_params=PARAMS, name=name, cost_estimate=cost,
        input_output_aliases=alias or {},
    )(*args)


def stay(x):
    return pltpu.with_memory_space_constraint(x, pltpu.HBM)


def first_call(where, offsets, groups, depth, measured, state, lead):
    coefs, sources = state.shape
    sensors, own = measured.shape
    total = 2 * own
    dma = pltpu.SemaphoreType.DMA((sources // BLOCK,))
    inputs = (offsets, jnp.asarray(windowed_cosines()), groups, depth, measured, state, lead)
    return call(
        first_kernel,
        "first_forward",
        [where] + [stay(x) for x in inputs],
        [
            struct(BF16, 2, coefs, total),
            struct(BF16, 2, total, coefs),
            struct(BF16, total, sensors),
            struct(jnp.int32, 3),
            struct(F32, own, sensors),
            struct(F32, 1, sources),
            struct(F32, coefs, sources),
            struct(BF16, sensors, sources),
        ],
        ins=[SMEM] + [HBM] * len(inputs),
        out_specs=[VMEM, VMEM, VMEM, SMEM, VMEM, VMEM, VMEM, VMEM],
        scratch=[
            pltpu.SMEM(offsets.shape, jnp.int32),
            pltpu.VMEM((4, K, K), BF16),
            pltpu.VMEM((1, sources), jnp.int32),
            pltpu.VMEM((sensors, own), F32),
            pltpu.VMEM((coefs, sensors), F32),
            dma,
            dma,
            pltpu.SemaphoreType.DMA((5,)),
        ],
    )


def step_call(marks, got, others, table, scale, depth, state, lead):
    coefs, sources = state.shape
    sensors = lead.shape[0]
    first, last = scale is None, others is not None
    args = [marks, got] + ([others] if last else []) + [table, depth, state, lead] + ([] if first else [scale])
    return call(
        lambda *refs: step_kernel(*refs, first=first, last=last, block=BLOCK),
        "step",
        args,
        [struct(F32, coefs, sources), struct(F32, 8, LANES)],
        ins=[SMEM] + [VMEM] * (len(args) - 1),
        scratch=[pltpu.VMEM((coefs, sensors), BF16)] + ([pltpu.VMEM((table.shape[2], sensors), BF16)] if last else []),
    )


def forward_call(marks, state, depth, lead, table_t, power, pair, tau):
    coefs, sources = state.shape
    sensors = lead.shape[0]
    return call(
        lambda *refs: forward_kernel(*refs, block=BLOCK, tau=tau),
        "forward",
        [marks, state, depth, lead, table_t, power, pair],
        [struct(F32, 3 * table_t.shape[1], sensors)],
        ins=[SMEM] + [VMEM] * 6,
        scratch=[pltpu.VMEM((2, 2 * coefs, GROUP), BF16)],
        cost=pl.CostEstimate(flops=4 * coefs * sources * sensors, bytes_accessed=8 << 20, transcendentals=0),
    )[0]


def estimate_call(marks, state, powers, tau, so_far=None):
    coefs, sources = state.shape
    blocks = sources // BLOCK
    middle = so_far is None
    args = [marks, state, *powers] + ([] if middle else [so_far])
    return call(
        lambda *refs: estimate_kernel(*refs, tau=tau, middle=middle),
        "estimate",
        args,
        [struct(F32, coefs, sources)],
        ins=[SMEM] + [VMEM] * (1 + len(powers)) + ([] if middle else [HBM]),
        out_specs=[HBM],
        scratch=[pltpu.VMEM((blocks, coefs, BLOCK), F32), pltpu.SemaphoreType.DMA((blocks,))],
        alias={} if middle else {len(args) - 1: 0},
        cost=pl.CostEstimate(flops=coefs * sources, bytes_accessed=4 << 20, transcendentals=0),
    )[0]


def shards(measured, lead_field, depth, coefficients, offsets, group_ids):
    sensors, own = measured.shape
    sources = lead_field.shape[1]
    frames = coefficients.shape[1]
    frm_count = lax.axis_size("frm")
    src_count = math.prod(AXES.values())
    total = own * frm_count
    coefs = frames * K
    tau = group_weight * math.sqrt(GROUP * frames * frm_count * K)
    where = jnp.stack([lax.axis_index("frm"), lax.axis_index(PLANE)])

    def exchange(rows, axes):
        return lax.all_to_all(rows, axes, 0, 0, tiled=True)

    def move(x, chips, cores):
        route = []
        for chip in range(src_count):
            for core in range(frm_count):
                to = (chip + chips) % src_count * frm_count + (core + cores) % frm_count
                route.append((chip * frm_count + core, to))
        return lax.ppermute(x, (*SRC, "frm"), route)

    state = coefficients.transpose(1, 2, 0).reshape(coefs, sources)
    table, table_t, folded, marks, rows, depth_row, state, lead = first_call(
        where, offsets, group_ids.reshape(1, sources), depth.reshape(1, sources), measured, state, lead_field
    )
    scale = None
    for iteration in range(ITERS):
        last = iteration == ITERS - 1
        plane = call(
            plane_kernel, "plane_sum", [exchange(folded, PLANES)], [struct(F32, 8 * AXES["z"], sensors)]
        )[0]
        slab = call(
            lambda *refs, last=last: owner_kernel(*refs, last=last),
            "owner",
            [marks, exchange(plane, "z"), rows],
            [struct(BF16, total, sensors)],
            ins=[SMEM, VMEM, VMEM],
        )[0]
        got = exchange(slab, PLANE if last else PLANES)
        others = move(got, 0, 1) if last else None
        state, power = step_call(marks, got, others, table, scale, depth_row, state, lead)
        pair = move(power, 0, 1)
        powers = [power, pair, move(power, 1, 0), move(power, 1, 1), move(power, -1, 0), move(power, -1, 1)]
        if not last:
            parts = forward_call(marks, state, depth_row, lead, table_t, power, pair, tau)
            folded, scale = call(
                lambda *refs: fold_kernel(*refs, tau=tau),
                "fold",
                [parts, *powers],
                [struct(BF16, total, sensors), struct(F32, 8, LANES)],
            )

    residual = call(residual_kernel, "residual", [got], [struct(F32, sensors, own)])[0]
    estimate = estimate_call(marks, state, powers[:2], tau)
    estimate = estimate_call(marks, state, powers, tau, estimate)
    return (estimate.reshape(frames, K, sources).transpose(2, 0, 1), residual)


def solution(mesh):
    fine = Mesh(mesh.devices.reshape(*AXES.values(), mesh.shape["frm"]), (*AXES, "frm"))
    return jax.shard_map(
        shards,
        mesh=fine,
        in_specs=(
            P(None, "frm"),
            P(None, SRC),
            P(SRC),
            P(SRC, "frm", None),
            P("frm"),
            P(SRC),
        ),
        out_specs=(P(SRC, "frm", None), P(None, "frm")),
        check_vma=False,
    )
```

```python
import math

import jax
import jax.numpy as jnp
import ml_dtypes
import numpy as np
from jax import lax
from jax.experimental import pallas as pl
from jax.experimental.pallas import tpu as pltpu
from jax.sharding import Mesh
from jax.sharding import PartitionSpec as P

K = 64
GROUP = 2048
ITERS = 3
LANES = 128
BLOCK = 512
step_size = 0.5
shrink_one = 0.05
group_weight = 0.03
epsilon = 1e-06

F32 = jnp.float32
BF16 = jnp.bfloat16
HIGHEST = lax.Precision.HIGHEST
PARAMS = pltpu.CompilerParams(vmem_limit_bytes=16 * 1024 * 1024)
AXES = {"x": 4, "z": 8, "y": 4}
SRC = ("x", "z", "y")
PLANE = ("x", "y")
PLANES = ("frm", "x", "y")


def windowed_cosines():
    t = np.arange(K)[:, None] + 0.5
    k = np.arange(K)[None, :] + 0.5
    wave = np.sin(np.pi * t / K) * np.sqrt(2.0 / K) * np.cos(np.pi * k * t / K)
    high = wave.astype(ml_dtypes.bfloat16)
    low = (wave - high.astype(np.float64)).astype(ml_dtypes.bfloat16)
    return np.stack([high, low, high.T, low.T])


def split(x):
    high = x.astype(BF16)
    return high, (x - high.astype(F32)).astype(BF16)


def dot(a, b):
    return jnp.dot(a, b, preferred_element_type=F32)


def dot_t(a, b):
    return lax.dot_general(a, b, (((1,), (1,)), ((), ())), preferred_element_type=F32)


def to_samples(atoms_ref, sums):
    high, low = split(sums)
    return dot(atoms_ref[0], high) + dot(atoms_ref[0], low) + dot(atoms_ref[1], high)


def group_scale(power, tau):
    return jnp.maximum(0.0, 1.0 - tau / jnp.sqrt(power + epsilon))


def scales_of(powers, tau):
    mine, pair, after, after_pair, before, before_pair = (ref[...] for ref in powers)
    chip = mine + pair
    return (
        group_scale(chip[0:1] + (before + before_pair)[2:3], tau),
        group_scale(chip[1:2], tau),
        group_scale(chip[2:3] + (after + after_pair)[0:1], tau),
    )


def first_kernel(
    where_ref, offsets_hbm, wave_hbm, group_hbm, depth_hbm, measured_hbm, coef_hbm, lead_hbm,
    table_ref, table_t_ref, out_ref, marks_ref, rows_ref, depth_ref, coef_ref, lead_ref,
    offsets_ref, wave_ref, group_ref, measured_ref, turned_ref, acc_ref, coef_sem, lead_sem, small_sem,
):
    total = table_ref.shape[2]
    sources = lead_ref.shape[1]
    blocks = lead_sem.shape[0]
    block = sources // blocks
    pairs = (
        (offsets_hbm, offsets_ref), (wave_hbm, wave_ref), (group_hbm, group_ref), (measured_hbm, measured_ref),
        (depth_hbm, depth_ref),
    )
    small = [pltpu.make_async_copy(a, b, small_sem.at[n]) for n, (a, b) in enumerate(pairs)]
    for load in small:
        load.start()
    loads = []
    for j in range(blocks):
        cols = slice(j * block, (j + 1) * block)
        loads.append(
            (
                pltpu.make_async_copy(lead_hbm.at[:, cols], lead_ref.at[:, cols], lead_sem.at[j]),
                pltpu.make_async_copy(coef_hbm.at[:, cols], coef_ref.at[:, cols], coef_sem.at[j]),
            )
        )
        for load in loads[-1]:
            load.start()
    for load in small:
        load.wait()

    groups = group_ref[...]
    edge = jnp.sum((groups == groups[0:1, 0:1]).astype(jnp.int32), axis=1, keepdims=True)
    marks_ref[0:1, :] = jnp.broadcast_to(edge, (1, LANES))
    marks_ref[1:2, :] = jnp.full((1, LANES), where_ref[0], jnp.int32)
    marks_ref[2:8, :] = jnp.zeros((6, LANES), jnp.int32)
    for t in range(measured_ref.shape[0] // LANES):
        lanes = slice(t * LANES, (t + 1) * LANES)
        turned_ref[:, lanes] = measured_ref[lanes, :].T
    rows_ref[...] = turned_ref[pl.ds(pl.multiple_of(where_ref[1] * 8, 8), 8), :]
    for f in range(offsets_ref.shape[0]):
        rows = slice(f * K, (f + 1) * K)
        for axis in range(2):
            shape = (total, K) if axis == 0 else (K, total)
            sample = lax.broadcasted_iota(jnp.int32, shape, axis)
            position = lax.broadcasted_iota(jnp.int32, shape, 1 - axis)
            delay = lax.rem(sample - offsets_ref[f] + total, total)
            placing = (delay == position).astype(F32).astype(BF16)
            for h in range(2):
                if axis == 0:
                    table_t_ref[h, :, rows] = dot(placing, wave_ref[h]).astype(BF16)
                else:
                    table_ref[h, rows, :] = dot(wave_ref[2 + h], placing).astype(BF16)

    for j in range(blocks):
        for load in loads[j]:
            load.wait()
        cols = slice(j * block, (j + 1) * block)
        part = dot_t((coef_ref[:, cols] * depth_ref[:, cols]).astype(BF16), lead_ref[:, cols])
        if j == 0:
            acc_ref[...] = part
        else:
            acc_ref[...] += part
    out_ref[...] = to_samples(table_t_ref, acc_ref[...]).astype(BF16)


def slabs(x):
    return [x[i : i + 8] for i in range(0, x.shape[0], 8)]


def step_kernel(
    marks_ref, got_ref, *rest, first, last, block
):
    if last:
        other_ref, *rest = rest
    table_ref, depth_ref, state_ref, lead_ref, *rest = rest
    if not first:
        scale_ref, *rest = rest
    new_ref, power_ref, turned_ref, *rest = rest
    sources = state_ref.shape[1]
    if last:
        (samples_ref,) = rest
        own = samples_ref.shape[0] // 2
        highs = [jnp.concatenate(slabs(ref[...].astype(F32))[::2], axis=0) for ref in (got_ref, other_ref)]
        first_core = marks_ref[1:2, 0:1] == 0
        samples_ref[:own] = jnp.where(first_core, *highs).astype(BF16)
        samples_ref[own:] = jnp.where(first_core, *highs[::-1]).astype(BF16)
    else:
        samples_ref = got_ref
    turned = dot(table_ref[0], samples_ref[...]) + dot(table_ref[1], samples_ref[...])
    turned_ref[...] = turned.astype(BF16)

    start = marks_ref[0:1, 0:1]
    bounds = (start, start + GROUP)
    scales = None if first else [scale_ref[g : g + 1, 0:1] for g in range(3)]
    sums = [jnp.zeros((1, block), F32) for _ in range(4)]
    for j in range(sources // block):
        cols = slice(j * block, (j + 1) * block)
        half = j * block // GROUP
        gradient = dot(turned_ref[...], lead_ref[:, cols])
        source = j * block + lax.broadcasted_iota(jnp.int32, (1, block), 1)
        before = source < bounds[half]
        state = state_ref[:, cols]
        if not first:
            state = state * jnp.where(before, scales[half], scales[half + 1])
        moved = state + (step_size * depth_ref[:, cols]) * gradient
        shrunk = moved - jnp.clip(moved, -shrink_one, shrink_one)
        new_ref[:, cols] = shrunk
        squares = jnp.sum(shrunk * shrunk, axis=0, keepdims=True)
        sums[2 * half] += jnp.where(before, squares, 0.0)
        sums[2 * half + 1] += jnp.where(before, 0.0, squares)
    power_ref[...] = jnp.zeros_like(power_ref)
    for g, total in enumerate((sums[0], sums[1] + sums[2], sums[3])):
        power_ref[g : g + 1, :] = jnp.broadcast_to(jnp.sum(total, axis=1, keepdims=True), (1, LANES))


def forward_kernel(
    marks_ref, state_ref, depth_ref, lead_ref, table_t_ref, power_ref, pair_ref, out_ref, weighted_ref, *,
    block, tau,
):
    coefs, sources = state_ref.shape
    total = out_ref.shape[0] // 3
    start = marks_ref[0:1, 0:1]
    bounds = (start, start + GROUP)
    none = jnp.zeros((), BF16)
    for j in range(sources // block):
        cols = slice(j * block, (j + 1) * block)
        half = j * block // GROUP
        before = j * block + lax.broadcasted_iota(jnp.int32, (1, block), 1) < bounds[half]
        weighted = (state_ref[:, cols] * depth_ref[:, cols]).astype(BF16)
        inner = slice(j * block - half * GROUP, (j + 1) * block - half * GROUP)
        weighted_ref[half, :coefs, inner] = jnp.where(before, weighted, none)
        weighted_ref[half, coefs:, inner] = jnp.where(before, none, weighted)
    halves = [dot_t(weighted_ref[h], lead_ref[:, h * GROUP : (h + 1) * GROUP]) for h in range(2)]
    middle = group_scale(power_ref[1:2, 0:1] + pair_ref[1:2, 0:1], tau) * (halves[0][coefs:] + halves[1][:coefs])
    parts = (halves[0][:coefs], middle, halves[1][coefs:])
    for g in range(3):
        out_ref[g * total : (g + 1) * total, :] = to_samples(table_t_ref, parts[g])


def fold_kernel(parts_ref, *rest, tau):
    *powers, out_ref, scale_ref = rest
    total = out_ref.shape[0]
    scale_ref[...] = jnp.zeros_like(scale_ref)
    scales = scales_of(powers, tau)
    for g, scale in enumerate(scales):
        scale_ref[g : g + 1, :] = scale
    first, middle, last = (parts_ref[g * total : (g + 1) * total, :] for g in range(3))
    out_ref[...] = (scales[0][:, 0:1] * first + middle + scales[2][:, 0:1] * last).astype(BF16)


def plane_kernel(got_ref, out_ref):
    total = sum(slabs(got_ref[...].astype(F32)))
    out_ref[...] = jnp.concatenate([total] * (out_ref.shape[0] // 8), axis=0).astype(BF16)


def owner_kernel(got_ref, measured_ref, out_ref, *, last):
    row = measured_ref[...] - sum(slabs(got_ref[...].astype(F32)))
    if last:
        high = row.astype(BF16).astype(F32)
        row = jnp.concatenate([high, row - high], axis=0)
    out_ref[...] = jnp.concatenate([row] * (out_ref.shape[0] // row.shape[0]), axis=0).astype(BF16)


def residual_kernel(own_ref, out_ref):
    pieces = slabs(own_ref[...].astype(F32))
    rows = jnp.concatenate([high + low for high, low in zip(pieces[::2], pieces[1::2])], axis=0)
    for t in range(out_ref.shape[0] // LANES):
        lanes = slice(t * LANES, (t + 1) * LANES)
        out_ref[lanes, :] = rows[:, lanes].T


def estimate_kernel(marks_ref, state_ref, *rest, tau, middle):
    if middle:
        power_ref, pair_ref, out_hbm, scaled_ref, sem = rest
        scales = [None, group_scale(power_ref[1:2, 0:1] + pair_ref[1:2, 0:1], tau), None]
    else:
        *powers, _, out_hbm, scaled_ref, sem = rest
        scales = [scale[:, 0:1] for scale in scales_of(powers, tau)]
    blocks, _, block = scaled_ref.shape
    start = jnp.max(marks_ref[0:1, :])
    bounds = (start, start + GROUP)
    wanted, stores = [], []
    for j in range(blocks):
        cols = slice(j * block, (j + 1) * block)
        half = j * block // GROUP
        inside = bounds[0] <= j * block if half == 0 else (j + 1) * block <= bounds[1]
        wanted.append(inside if middle else jnp.logical_not(inside))
        stores.append(pltpu.make_async_copy(scaled_ref.at[j], out_hbm.at[:, cols], sem.at[j]))

        @pl.when(wanted[j])
        def _():
            if middle:
                scale = scales[1]
            else:
                before = j * block + lax.broadcasted_iota(jnp.int32, (1, block), 1) < bounds[half]
                scale = jnp.where(before, scales[half], scales[half + 1])
            scaled_ref[j] = state_ref[:, cols] * scale
            stores[j].start()

    for j in range(blocks):
        pl.when(wanted[j])(stores[j].wait)


SMEM = pl.BlockSpec(memory_space=pltpu.SMEM)
VMEM = pl.BlockSpec(memory_space=pltpu.VMEM)
HBM = pl.BlockSpec(memory_space=pltpu.HBM)


def struct(dtype, *shape):
    return jax.ShapeDtypeStruct(shape, dtype)


def call(kernel, name, args, outs, *, ins=None, out_specs=None, scratch=(), cost=None, alias=None):
    return pl.pallas_call(
        kernel, in_specs=ins or [VMEM] * len(args), out_specs=out_specs or [VMEM] * len(outs), out_shape=outs,
        scratch_shapes=list(scratch), compiler_params=PARAMS, name=name, cost_estimate=cost,
        input_output_aliases=alias or {},
    )(*args)


def stay(x):
    return pltpu.with_memory_space_constraint(x, pltpu.HBM)


def first_call(where, offsets, groups, depth, measured, state, lead):
    coefs, sources = state.shape
    sensors, own = measured.shape
    total = 2 * own
    dma = pltpu.SemaphoreType.DMA((sources // BLOCK,))
    inputs = (offsets, jnp.asarray(windowed_cosines()), groups, depth, measured, state, lead)
    return call(
        first_kernel,
        "first_forward",
        [where] + [stay(x) for x in inputs],
        [
            struct(BF16, 2, coefs, total),
            struct(BF16, 2, total, coefs),
            struct(BF16, total, sensors),
            struct(jnp.int32, 8, LANES),
            struct(F32, 8, sensors),
            struct(F32, 1, sources),
            struct(F32, coefs, sources),
            struct(BF16, sensors, sources),
        ],
        ins=[SMEM] + [HBM] * len(inputs),
                scratch=[
            pltpu.SMEM(offsets.shape, jnp.int32),
            pltpu.VMEM((4, K, K), BF16),
            pltpu.VMEM((1, sources), jnp.int32),
            pltpu.VMEM((sensors, own), F32),
            pltpu.VMEM((own, sensors), F32),
            pltpu.VMEM((coefs, sensors), F32),
            dma,
            dma,
            pltpu.SemaphoreType.DMA((5,)),
        ],
    )


def step_call(marks, got, others, table, scale, depth, state, lead):
    coefs, sources = state.shape
    sensors = lead.shape[0]
    first, last = scale is None, others is not None
    args = [marks, got] + ([others] if last else []) + [table, depth, state, lead] + ([] if first else [scale])
    return call(
        lambda *refs: step_kernel(*refs, first=first, last=last, block=BLOCK),
        "step",
        args,
        [struct(F32, coefs, sources), struct(F32, 8, LANES)],
        scratch=[pltpu.VMEM((coefs, sensors), BF16)] + ([pltpu.VMEM((table.shape[2], sensors), BF16)] if last else []),
    )


def forward_call(marks, state, depth, lead, table_t, power, pair, tau):
    coefs, sources = state.shape
    sensors = lead.shape[0]
    return call(
        lambda *refs: forward_kernel(*refs, block=BLOCK, tau=tau),
        "forward",
        [marks, state, depth, lead, table_t, power, pair],
        [struct(F32, 3 * table_t.shape[1], sensors)],
        scratch=[pltpu.VMEM((2, 2 * coefs, GROUP), BF16)],
        cost=pl.CostEstimate(flops=4 * coefs * sources * sensors, bytes_accessed=8 << 20, transcendentals=0),
    )[0]


def estimate_call(marks, state, powers, tau, so_far=None):
    coefs, sources = state.shape
    blocks = sources // BLOCK
    middle = so_far is None
    args = [marks, state, *powers] + ([] if middle else [so_far])
    return call(
        lambda *refs: estimate_kernel(*refs, tau=tau, middle=middle),
        "estimate",
        args,
        [struct(F32, coefs, sources)],
        ins=[VMEM] * (2 + len(powers)) + ([] if middle else [HBM]),
        out_specs=[HBM],
        scratch=[pltpu.VMEM((blocks, coefs, BLOCK), F32), pltpu.SemaphoreType.DMA((blocks,))],
        alias={} if middle else {len(args) - 1: 0},
        cost=pl.CostEstimate(flops=coefs * sources, bytes_accessed=4 << 20, transcendentals=0),
    )[0]


def shards(measured, lead_field, depth, coefficients, offsets, group_ids):
    sensors, own = measured.shape
    sources = lead_field.shape[1]
    frames = coefficients.shape[1]
    frm_count = lax.axis_size("frm")
    src_count = math.prod(AXES.values())
    total = own * frm_count
    coefs = frames * K
    tau = group_weight * math.sqrt(GROUP * frames * frm_count * K)
    where = jnp.stack([lax.axis_index("frm"), lax.axis_index(PLANE)])

    def exchange(rows, axes):
        return lax.all_to_all(rows, axes, 0, 0, tiled=True)

    def move(x, chips, cores):
        route = []
        for chip in range(src_count):
            for core in range(frm_count):
                to = (chip + chips) % src_count * frm_count + (core + cores) % frm_count
                route.append((chip * frm_count + core, to))
        return lax.ppermute(x, (*SRC, "frm"), route)

    state = coefficients.transpose(1, 2, 0).reshape(coefs, sources)
    table, table_t, folded, marks, rows, depth_row, state, lead = first_call(
        where, offsets, group_ids.reshape(1, sources), depth.reshape(1, sources), measured, state, lead_field
    )
    scale = None
    for iteration in range(ITERS):
        last = iteration == ITERS - 1
        plane = call(
            plane_kernel, "plane_sum", [exchange(folded, PLANES)], [struct(BF16, 8 * AXES["z"], sensors)]
        )[0]
        slab = call(
            lambda *refs, last=last: owner_kernel(*refs, last=last),
            "owner",
            [exchange(plane, "z"), rows],
            [struct(BF16, total, sensors)],
        )[0]
        got = exchange(slab, PLANE if last else PLANES)
        others = move(got, 0, 1) if last else None
        state, power = step_call(marks, got, others, table, scale, depth_row, state, lead)
        pair = move(power, 0, 1)
        powers = [power, pair, move(power, -1, 0), move(power, -1, 1), move(power, 1, 0), move(power, 1, 1)]
        if last:
            residual = call(residual_kernel, "residual", [got], [struct(F32, sensors, own)])[0]
            estimate = estimate_call(marks, state, [power, pair], tau)
        else:
            parts = forward_call(marks, state, depth_row, lead, table_t, power, pair, tau)
        if not last:
            folded, scale = call(
                lambda *refs: fold_kernel(*refs, tau=tau),
                "fold",
                [parts, *powers],
                [struct(BF16, total, sensors), struct(F32, 8, LANES)],
            )

    estimate = estimate_call(marks, state, powers, tau, estimate)
    return (estimate.reshape(frames, K, sources).transpose(2, 0, 1), residual)


def solution(mesh):
    fine = Mesh(mesh.devices.reshape(*AXES.values(), mesh.shape["frm"]), (*AXES, "frm"))
    return jax.shard_map(
        shards,
        mesh=fine,
        in_specs=(
            P(None, "frm"),
            P(None, SRC),
            P(SRC),
            P(SRC, "frm", None),
            P("frm"),
            P(SRC),
        ),
        out_specs=(P(SRC, "frm", None), P(None, "frm")),
        check_vma=False,
    )
```

```python
import math

import jax
import jax.numpy as jnp
import ml_dtypes
import numpy as np
from jax import lax
from jax.experimental import pallas as pl
from jax.experimental.pallas import tpu as pltpu
from jax.sharding import Mesh
from jax.sharding import PartitionSpec as P

K = 64
GROUP = 2048
ITERS = 3
LANES = 128
BLOCK = 512
FIRST_BLOCK = 2048
step_size = 0.5
shrink_one = 0.05
group_weight = 0.03
epsilon = 1e-06

F32 = jnp.float32
BF16 = jnp.bfloat16
HIGHEST = lax.Precision.HIGHEST
PARAMS = pltpu.CompilerParams(vmem_limit_bytes=16 * 1024 * 1024)
AXES = {"x": 4, "z": 8, "y": 4}
SRC = ("x", "z", "y")
PLANE = ("x", "y")
PLANES = ("frm", "x", "y")


def windowed_cosines():
    t = np.arange(K)[:, None] + 0.5
    k = np.arange(K)[None, :] + 0.5
    wave = np.sin(np.pi * t / K) * np.sqrt(2.0 / K) * np.cos(np.pi * k * t / K)
    high = wave.astype(ml_dtypes.bfloat16)
    low = (wave - high.astype(np.float64)).astype(ml_dtypes.bfloat16)
    return np.stack([high, low, high.T, low.T])


def split(x):
    high = x.astype(BF16)
    return high, (x - high.astype(F32)).astype(BF16)


def dot(a, b):
    return jnp.dot(a, b, preferred_element_type=F32)


def dot_t(a, b):
    return lax.dot_general(a, b, (((1,), (1,)), ((), ())), preferred_element_type=F32)


def to_samples(atoms_ref, sums):
    high, low = split(sums)
    return dot(atoms_ref[0], high) + dot(atoms_ref[0], low) + dot(atoms_ref[1], high)


def group_scale(power, tau):
    return jnp.maximum(0.0, 1.0 - tau / jnp.sqrt(power + epsilon))


def scales_of(powers, tau):
    chip, after, before = (ref[...] for ref in powers)
    return (
        group_scale(chip[0:1] + before[2:3], tau),
        group_scale(chip[1:2], tau),
        group_scale(chip[2:3] + after[0:1], tau),
    )


def first_kernel(
    where_ref, offsets_hbm, wave_hbm, group_hbm, depth_hbm, measured_hbm, coef_hbm, lead_hbm,
    table_ref, table_t_ref, out_ref, marks_ref, rows_ref, depth_ref, coef_ref, lead_ref,
    offsets_ref, wave_ref, group_ref, measured_ref, turned_ref, acc_ref, coef_sem, lead_sem, small_sem,
):
    total = table_ref.shape[2]
    sources = lead_ref.shape[1]
    blocks = lead_sem.shape[0]
    block = sources // blocks
    pairs = (
        (offsets_hbm, offsets_ref), (wave_hbm, wave_ref), (group_hbm, group_ref), (measured_hbm, measured_ref),
        (depth_hbm, depth_ref),
    )
    small = [pltpu.make_async_copy(a, b, small_sem.at[n]) for n, (a, b) in enumerate(pairs)]
    for load in small:
        load.start()
    loads = []
    for j in range(blocks):
        cols = slice(j * block, (j + 1) * block)
        loads.append(
            (
                pltpu.make_async_copy(lead_hbm.at[:, cols], lead_ref.at[:, cols], lead_sem.at[j]),
                pltpu.make_async_copy(coef_hbm.at[:, cols], coef_ref.at[:, cols], coef_sem.at[j]),
            )
        )
        for load in loads[-1]:
            load.start()
    for load in small:
        load.wait()

    groups = group_ref[...]
    edge = jnp.sum((groups == groups[0:1, 0:1]).astype(jnp.int32), axis=1, keepdims=True)
    marks_ref[0:1, :] = jnp.broadcast_to(edge, (1, LANES))
    marks_ref[1:2, :] = jnp.full((1, LANES), where_ref[0], jnp.int32)
    marks_ref[2:8, :] = jnp.zeros((6, LANES), jnp.int32)
    for t in range(measured_ref.shape[0] // LANES):
        lanes = slice(t * LANES, (t + 1) * LANES)
        turned_ref[:, lanes] = measured_ref[lanes, :].T
    rows_ref[...] = turned_ref[pl.ds(pl.multiple_of(where_ref[1] * 8, 8), 8), :]
    for f in range(offsets_ref.shape[0]):
        rows = slice(f * K, (f + 1) * K)
        for axis in range(2):
            shape = (total, K) if axis == 0 else (K, total)
            sample = lax.broadcasted_iota(jnp.int32, shape, axis)
            position = lax.broadcasted_iota(jnp.int32, shape, 1 - axis)
            delay = lax.rem(sample - offsets_ref[f] + total, total)
            placing = (delay == position).astype(F32).astype(BF16)
            for h in range(2):
                if axis == 0:
                    table_t_ref[h, :, rows] = dot(placing, wave_ref[h]).astype(BF16)
                else:
                    table_ref[h, rows, :] = dot(wave_ref[2 + h], placing).astype(BF16)

    for j in range(blocks):
        for load in loads[j]:
            load.wait()
        cols = slice(j * block, (j + 1) * block)
        part = dot_t((coef_ref[:, cols] * depth_ref[:, cols]).astype(BF16), lead_ref[:, cols])
        if j == 0:
            acc_ref[...] = part
        else:
            acc_ref[...] += part
    out_ref[...] = to_samples(table_t_ref, acc_ref[...]).astype(BF16)


def slabs(x):
    return [x[i : i + 8] for i in range(0, x.shape[0], 8)]


def step_kernel(
    marks_ref, got_ref, *rest, first, last, block
):
    if last:
        other_ref, *rest = rest
    table_ref, depth_ref, state_ref, lead_ref, *rest = rest
    if not first:
        scale_ref, *rest = rest
    new_ref, power_ref, turned_ref, *rest = rest
    sources = state_ref.shape[1]
    if last:
        (samples_ref,) = rest
        own = samples_ref.shape[0] // 2
        highs = [jnp.concatenate(slabs(ref[...].astype(F32))[::2], axis=0) for ref in (got_ref, other_ref)]
        first_core = marks_ref[1:2, 0:1] == 0
        samples_ref[:own] = jnp.where(first_core, *highs).astype(BF16)
        samples_ref[own:] = jnp.where(first_core, *highs[::-1]).astype(BF16)
    else:
        samples_ref = got_ref
    turned = dot(table_ref[0], samples_ref[...]) + dot(table_ref[1], samples_ref[...])
    turned_ref[...] = turned.astype(BF16)

    start = marks_ref[0:1, 0:1]
    bounds = (start, start + GROUP)
    scales = None if first else [scale_ref[g : g + 1, 0:1] for g in range(3)]
    sums = [jnp.zeros((1, block), F32) for _ in range(4)]
    for j in range(sources // block):
        cols = slice(j * block, (j + 1) * block)
        half = j * block // GROUP
        gradient = dot(turned_ref[...], lead_ref[:, cols])
        source = j * block + lax.broadcasted_iota(jnp.int32, (1, block), 1)
        before = source < bounds[half]
        state = state_ref[:, cols]
        if not first:
            state = state * jnp.where(before, scales[half], scales[half + 1])
        moved = state + (step_size * depth_ref[:, cols]) * gradient
        shrunk = moved - jnp.clip(moved, -shrink_one, shrink_one)
        new_ref[:, cols] = shrunk
        squares = jnp.sum(shrunk * shrunk, axis=0, keepdims=True)
        sums[2 * half] += jnp.where(before, squares, 0.0)
        sums[2 * half + 1] += jnp.where(before, 0.0, squares)
    power_ref[...] = jnp.zeros_like(power_ref)
    for g, total in enumerate((sums[0], sums[1] + sums[2], sums[3])):
        power_ref[g : g + 1, :] = jnp.broadcast_to(jnp.sum(total, axis=1, keepdims=True), (1, LANES))


def forward_kernel(
    marks_ref, state_ref, depth_ref, lead_ref, table_t_ref, chip_ref, out_ref, weighted_ref, *,
    block, tau,
):
    coefs, sources = state_ref.shape
    total = out_ref.shape[0] // 3
    start = marks_ref[0:1, 0:1]
    bounds = (start, start + GROUP)
    none = jnp.zeros((), BF16)
    for j in range(sources // block):
        cols = slice(j * block, (j + 1) * block)
        half = j * block // GROUP
        before = j * block + lax.broadcasted_iota(jnp.int32, (1, block), 1) < bounds[half]
        weighted = (state_ref[:, cols] * depth_ref[:, cols]).astype(BF16)
        inner = slice(j * block - half * GROUP, (j + 1) * block - half * GROUP)
        weighted_ref[half, :coefs, inner] = jnp.where(before, weighted, none)
        weighted_ref[half, coefs:, inner] = jnp.where(before, none, weighted)
    halves = [dot_t(weighted_ref[h], lead_ref[:, h * GROUP : (h + 1) * GROUP]) for h in range(2)]
    middle = group_scale(chip_ref[1:2, 0:1], tau) * (halves[0][coefs:] + halves[1][:coefs])
    parts = (halves[0][:coefs], middle, halves[1][coefs:])
    for g in range(3):
        out_ref[g * total : (g + 1) * total, :] = to_samples(table_t_ref, parts[g])


def fold_kernel(parts_ref, *rest, tau):
    *powers, out_ref, scale_ref = rest
    total = out_ref.shape[0]
    scale_ref[...] = jnp.zeros_like(scale_ref)
    scales = scales_of(powers, tau)
    for g, scale in enumerate(scales):
        scale_ref[g : g + 1, :] = scale
    first, middle, last = (parts_ref[g * total : (g + 1) * total, :] for g in range(3))
    out_ref[...] = (scales[0][:, 0:1] * first + middle + scales[2][:, 0:1] * last).astype(BF16)


def plane_kernel(got_ref, out_ref):
    total = sum(slabs(got_ref[...].astype(F32)))
    out_ref[...] = jnp.concatenate([total] * (out_ref.shape[0] // 8), axis=0).astype(BF16)


def owner_kernel(got_ref, measured_ref, out_ref, *, last):
    row = measured_ref[...] - sum(slabs(got_ref[...].astype(F32)))
    if last:
        high = row.astype(BF16).astype(F32)
        row = jnp.concatenate([high, row - high], axis=0)
    out_ref[...] = jnp.concatenate([row] * (out_ref.shape[0] // row.shape[0]), axis=0).astype(BF16)


def add_kernel(a_ref, b_ref, out_ref):
    out_ref[...] = a_ref[...] + b_ref[...]


def residual_kernel(own_ref, out_ref):
    pieces = slabs(own_ref[...].astype(F32))
    rows = jnp.concatenate([high + low for high, low in zip(pieces[::2], pieces[1::2])], axis=0)
    for t in range(out_ref.shape[0] // LANES):
        lanes = slice(t * LANES, (t + 1) * LANES)
        out_ref[lanes, :] = rows[:, lanes].T


def estimate_kernel(marks_ref, state_ref, *rest, tau, middle):
    if middle:
        chip_ref, out_hbm, scaled_ref, sem = rest
        scales = [None, group_scale(chip_ref[1:2, 0:1], tau), None]
    else:
        *powers, _, out_hbm, scaled_ref, sem = rest
        scales = [scale[:, 0:1] for scale in scales_of(powers, tau)]
    blocks, _, block = scaled_ref.shape
    start = jnp.max(marks_ref[0:1, :])
    bounds = (start, start + GROUP)
    wanted, stores = [], []
    for j in range(blocks):
        cols = slice(j * block, (j + 1) * block)
        half = j * block // GROUP
        inside = bounds[0] <= j * block if half == 0 else (j + 1) * block <= bounds[1]
        wanted.append(inside if middle else jnp.logical_not(inside))
        stores.append(pltpu.make_async_copy(scaled_ref.at[j], out_hbm.at[:, cols], sem.at[j]))

        @pl.when(wanted[j])
        def _():
            if middle:
                scale = scales[1]
            else:
                before = j * block + lax.broadcasted_iota(jnp.int32, (1, block), 1) < bounds[half]
                scale = jnp.where(before, scales[half], scales[half + 1])
            scaled_ref[j] = state_ref[:, cols] * scale
            stores[j].start()

    for j in range(blocks):
        pl.when(wanted[j])(stores[j].wait)


SMEM = pl.BlockSpec(memory_space=pltpu.SMEM)
VMEM = pl.BlockSpec(memory_space=pltpu.VMEM)
HBM = pl.BlockSpec(memory_space=pltpu.HBM)


def struct(dtype, *shape):
    return jax.ShapeDtypeStruct(shape, dtype)


def call(kernel, name, args, outs, *, ins=None, out_specs=None, scratch=(), cost=None, alias=None):
    return pl.pallas_call(
        kernel, in_specs=ins or [VMEM] * len(args), out_specs=out_specs or [VMEM] * len(outs), out_shape=outs,
        scratch_shapes=list(scratch), compiler_params=PARAMS, name=name, cost_estimate=cost,
        input_output_aliases=alias or {},
    )(*args)


def stay(x):
    return pltpu.with_memory_space_constraint(x, pltpu.HBM)


def first_call(where, offsets, groups, depth, measured, state, lead):
    coefs, sources = state.shape
    sensors, own = measured.shape
    total = 2 * own
    dma = pltpu.SemaphoreType.DMA((sources // FIRST_BLOCK,))
    inputs = (offsets, jnp.asarray(windowed_cosines()), groups, depth, measured, state, lead)
    return call(
        first_kernel,
        "first_forward",
        [where] + [stay(x) for x in inputs],
        [
            struct(BF16, 2, coefs, total),
            struct(BF16, 2, total, coefs),
            struct(BF16, total, sensors),
            struct(jnp.int32, 8, LANES),
            struct(F32, 8, sensors),
            struct(F32, 1, sources),
            struct(F32, coefs, sources),
            struct(BF16, sensors, sources),
        ],
        ins=[SMEM] + [HBM] * len(inputs),
                scratch=[
            pltpu.SMEM(offsets.shape, jnp.int32),
            pltpu.VMEM((4, K, K), BF16),
            pltpu.VMEM((1, sources), jnp.int32),
            pltpu.VMEM((sensors, own), F32),
            pltpu.VMEM((own, sensors), F32),
            pltpu.VMEM((coefs, sensors), F32),
            dma,
            dma,
            pltpu.SemaphoreType.DMA((5,)),
        ],
    )


def step_call(marks, got, others, table, scale, depth, state, lead):
    coefs, sources = state.shape
    sensors = lead.shape[0]
    first, last = scale is None, others is not None
    args = [marks, got] + ([others] if last else []) + [table, depth, state, lead] + ([] if first else [scale])
    return call(
        lambda *refs: step_kernel(*refs, first=first, last=last, block=BLOCK),
        "step",
        args,
        [struct(F32, coefs, sources), struct(F32, 8, LANES)],
        scratch=[pltpu.VMEM((coefs, sensors), BF16)] + ([pltpu.VMEM((table.shape[2], sensors), BF16)] if last else []),
    )


def forward_call(marks, state, depth, lead, table_t, chip, tau):
    coefs, sources = state.shape
    sensors = lead.shape[0]
    return call(
        lambda *refs: forward_kernel(*refs, block=BLOCK, tau=tau),
        "forward",
        [marks, state, depth, lead, table_t, chip],
        [struct(F32, 3 * table_t.shape[1], sensors)],
        scratch=[pltpu.VMEM((2, 2 * coefs, GROUP), BF16)],
        cost=pl.CostEstimate(flops=4 * coefs * sources * sensors, bytes_accessed=8 << 20, transcendentals=0),
    )[0]


def estimate_call(marks, state, powers, tau, so_far=None):
    coefs, sources = state.shape
    blocks = sources // BLOCK
    middle = so_far is None
    args = [marks, state, *powers] + ([] if middle else [so_far])
    return call(
        lambda *refs: estimate_kernel(*refs, tau=tau, middle=middle),
        "estimate",
        args,
        [struct(F32, coefs, sources)],
        ins=[VMEM] * (2 + len(powers)) + ([] if middle else [HBM]),
        out_specs=[HBM],
        scratch=[pltpu.VMEM((blocks, coefs, BLOCK), F32), pltpu.SemaphoreType.DMA((blocks,))],
        alias={} if middle else {len(args) - 1: 0},
        cost=pl.CostEstimate(flops=coefs * sources, bytes_accessed=4 << 20, transcendentals=0),
    )[0]


def shards(measured, lead_field, depth, coefficients, offsets, group_ids):
    sensors, own = measured.shape
    sources = lead_field.shape[1]
    frames = coefficients.shape[1]
    frm_count = lax.axis_size("frm")
    src_count = math.prod(AXES.values())
    total = own * frm_count
    coefs = frames * K
    tau = group_weight * math.sqrt(GROUP * frames * frm_count * K)
    where = jnp.stack([lax.axis_index("frm"), lax.axis_index(PLANE)])

    def exchange(rows, axes):
        return lax.all_to_all(rows, axes, 0, 0, tiled=True)

    def move(x, chips, cores):
        route = []
        for chip in range(src_count):
            for core in range(frm_count):
                to = (chip + chips) % src_count * frm_count + (core + cores) % frm_count
                route.append((chip * frm_count + core, to))
        return lax.ppermute(x, (*SRC, "frm"), route)

    state = coefficients.transpose(1, 2, 0).reshape(coefs, sources)
    table, table_t, folded, marks, rows, depth_row, state, lead = first_call(
        where, offsets, group_ids.reshape(1, sources), depth.reshape(1, sources), measured, state, lead_field
    )
    scale = None
    for iteration in range(ITERS):
        last = iteration == ITERS - 1
        plane = call(
            plane_kernel, "plane_sum", [exchange(folded, PLANES)], [struct(BF16, 8 * AXES["z"], sensors)]
        )[0]
        slab = call(
            lambda *refs, last=last: owner_kernel(*refs, last=last),
            "owner",
            [exchange(plane, "z"), rows],
            [struct(BF16, total, sensors)],
        )[0]
        got = exchange(slab, PLANE if last else PLANES)
        others = move(got, 0, 1) if last else None
        state, power = step_call(marks, got, others, table, scale, depth_row, state, lead)
        pair = move(power, 0, 1)
        chip = call(add_kernel, "chip_power", [power, pair], [struct(F32, 8, LANES)])[0]
        powers = [chip, move(chip, -1, 0), move(chip, 1, 0)]
        if last:
            residual = call(residual_kernel, "residual", [got], [struct(F32, sensors, own)])[0]
            estimate = estimate_call(marks, state, [chip], tau)
        else:
            parts = forward_call(marks, state, depth_row, lead, table_t, chip, tau)
        if not last:
            folded, scale = call(
                lambda *refs: fold_kernel(*refs, tau=tau),
                "fold",
                [parts, *powers],
                [struct(BF16, total, sensors), struct(F32, 8, LANES)],
            )

    estimate = estimate_call(marks, state, powers, tau, estimate)
    return (estimate.reshape(frames, K, sources).transpose(2, 0, 1), residual)


def solution(mesh):
    fine = Mesh(mesh.devices.reshape(*AXES.values(), mesh.shape["frm"]), (*AXES, "frm"))
    return jax.shard_map(
        shards,
        mesh=fine,
        in_specs=(
            P(None, "frm"),
            P(None, SRC),
            P(SRC),
            P(SRC, "frm", None),
            P("frm"),
            P(SRC),
        ),
        out_specs=(P(SRC, "frm", None), P(None, "frm")),
        check_vma=False,
    )
```

```python
import math

import jax
import jax.numpy as jnp
import ml_dtypes
import numpy as np
from jax import lax
from jax.experimental import pallas as pl
from jax.experimental.pallas import tpu as pltpu
from jax.sharding import Mesh
from jax.sharding import PartitionSpec as P

K = 64
GROUP = 2048
ITERS = 3
LANES = 128
BLOCK = 512
FIRST_BLOCK = 2048
SPILL = 64
step_size = 0.5
shrink_one = 0.05
group_weight = 0.03
epsilon = 1e-06

F32 = jnp.float32
BF16 = jnp.bfloat16
HIGHEST = lax.Precision.HIGHEST
PARAMS = pltpu.CompilerParams(vmem_limit_bytes=16 * 1024 * 1024)
AXES = {"x": 4, "z": 8, "y": 4}
SRC = ("x", "z", "y")
PLANE = ("x", "y")
PLANES = ("frm", "x", "y")


def windowed_cosines():
    t = np.arange(K)[:, None] + 0.5
    k = np.arange(K)[None, :] + 0.5
    wave = np.sin(np.pi * t / K) * np.sqrt(2.0 / K) * np.cos(np.pi * k * t / K)
    high = wave.astype(ml_dtypes.bfloat16)
    low = (wave - high.astype(np.float64)).astype(ml_dtypes.bfloat16)
    return np.stack([high, low, high.T, low.T])


def split(x):
    high = x.astype(BF16)
    return high, (x - high.astype(F32)).astype(BF16)


def dot(a, b):
    return jnp.dot(a, b, preferred_element_type=F32)


def dot_t(a, b):
    return lax.dot_general(a, b, (((1,), (1,)), ((), ())), preferred_element_type=F32)


def to_samples(atoms_ref, sums):
    high, low = split(sums)
    return dot(atoms_ref[0], high) + dot(atoms_ref[0], low) + dot(atoms_ref[1], high)


def group_scale(power, tau):
    return jnp.maximum(0.0, 1.0 - tau / jnp.sqrt(power + epsilon))


def scales_of(powers, tau):
    chip, one, two, core = (ref[...] for ref in powers)
    core = core[1:2, :]
    before, after = jnp.where(core == 0, one, two), jnp.where(core == 0, two, one)
    return (
        group_scale(chip[0:1] + before[2:3], tau),
        group_scale(chip[1:2], tau),
        group_scale(chip[2:3] + after[0:1], tau),
    )


def first_kernel(
    where_ref, offsets_hbm, wave_hbm, group_hbm, depth_hbm, measured_hbm, coef_hbm, lead_hbm,
    table_ref, table_t_ref, out_ref, marks_ref, rows_ref, depth_ref, coef_ref, lead_ref,
    offsets_ref, wave_ref, group_ref, measured_ref, turned_ref, acc_ref, coef_sem, lead_sem, small_sem,
):
    total = table_ref.shape[2]
    sources = lead_ref.shape[1]
    blocks = lead_sem.shape[0]
    block = sources // blocks
    pairs = (
        (offsets_hbm, offsets_ref), (wave_hbm, wave_ref), (group_hbm, group_ref), (measured_hbm, measured_ref),
        (depth_hbm, depth_ref),
    )
    small = [pltpu.make_async_copy(a, b, small_sem.at[n]) for n, (a, b) in enumerate(pairs)]
    for load in small:
        load.start()
    loads = []
    for j in range(blocks):
        cols = slice(j * block, (j + 1) * block)
        loads.append(
            (
                pltpu.make_async_copy(lead_hbm.at[:, cols], lead_ref.at[:, cols], lead_sem.at[j]),
                pltpu.make_async_copy(coef_hbm.at[:, cols], coef_ref.at[:, cols], coef_sem.at[j]),
            )
        )
        for load in loads[-1]:
            load.start()
    for load in small:
        load.wait()

    groups = group_ref[...]
    edge = jnp.sum((groups == groups[0:1, 0:1]).astype(jnp.int32), axis=1, keepdims=True)
    marks_ref[0:1, :] = jnp.broadcast_to(edge, (1, LANES))
    marks_ref[1:2, :] = jnp.full((1, LANES), where_ref[0], jnp.int32)
    marks_ref[2:8, :] = jnp.zeros((6, LANES), jnp.int32)
    for t in range(measured_ref.shape[0] // LANES):
        lanes = slice(t * LANES, (t + 1) * LANES)
        turned_ref[:, lanes] = measured_ref[lanes, :].T
    rows_ref[...] = turned_ref[pl.ds(pl.multiple_of(where_ref[1] * 8, 8), 8), :]
    for f in range(offsets_ref.shape[0]):
        rows = slice(f * K, (f + 1) * K)
        for axis in range(2):
            shape = (total, K) if axis == 0 else (K, total)
            sample = lax.broadcasted_iota(jnp.int32, shape, axis)
            position = lax.broadcasted_iota(jnp.int32, shape, 1 - axis)
            delay = lax.rem(sample - offsets_ref[f] + total, total)
            placing = (delay == position).astype(F32).astype(BF16)
            for h in range(2):
                if axis == 0:
                    table_t_ref[h, :, rows] = dot(placing, wave_ref[h]).astype(BF16)
                else:
                    table_ref[h, rows, :] = dot(wave_ref[2 + h], placing).astype(BF16)

    for j in range(blocks):
        for load in loads[j]:
            load.wait()
        cols = slice(j * block, (j + 1) * block)
        part = dot_t((coef_ref[:, cols] * depth_ref[:, cols]).astype(BF16), lead_ref[:, cols])
        if j == 0:
            acc_ref[...] = part
        else:
            acc_ref[...] += part
    out_ref[...] = to_samples(table_t_ref, acc_ref[...]).astype(BF16)


def slabs(x):
    return [x[i : i + 8] for i in range(0, x.shape[0], 8)]


def step_kernel(
    marks_ref, got_ref, *rest, first, last, block
):
    if last:
        other_ref, *rest = rest
    table_ref, depth_ref, state_ref, lead_ref, *rest = rest
    if not first:
        scale_ref, *rest = rest
    new_ref, power_ref, turned_ref, *rest = rest
    sources = state_ref.shape[1]
    if last:
        (samples_ref,) = rest
        own = samples_ref.shape[0] // 2
        highs = [jnp.concatenate(slabs(ref[...].astype(F32))[::2], axis=0) for ref in (got_ref, other_ref)]
        first_core = marks_ref[1:2, 0:1] == 0
        samples_ref[:own] = jnp.where(first_core, *highs).astype(BF16)
        samples_ref[own:] = jnp.where(first_core, *highs[::-1]).astype(BF16)
    else:
        samples_ref = got_ref
    turned = dot(table_ref[0], samples_ref[...]) + dot(table_ref[1], samples_ref[...])
    turned_ref[...] = turned.astype(BF16)

    start = marks_ref[0:1, 0:1]
    bounds = (start, start + GROUP)
    scales = None if first else [scale_ref[g : g + 1, 0:1] for g in range(3)]
    sums = [jnp.zeros((1, block), F32) for _ in range(4)]
    for j in range(sources // block):
        cols = slice(j * block, (j + 1) * block)
        half = j * block // GROUP
        gradient = dot(turned_ref[...], lead_ref[:, cols])
        source = j * block + lax.broadcasted_iota(jnp.int32, (1, block), 1)
        before = source < bounds[half]
        state = state_ref[:, cols]
        if not first:
            state = state * jnp.where(before, scales[half], scales[half + 1])
        moved = state + (step_size * depth_ref[:, cols]) * gradient
        shrunk = moved - jnp.clip(moved, -shrink_one, shrink_one)
        new_ref[:, cols] = shrunk
        squares = jnp.sum(shrunk * shrunk, axis=0, keepdims=True)
        sums[2 * half] += jnp.where(before, squares, 0.0)
        sums[2 * half + 1] += jnp.where(before, 0.0, squares)
    power_ref[...] = jnp.zeros_like(power_ref)
    for g, total in enumerate((sums[0], sums[1] + sums[2], sums[3])):
        power_ref[g : g + 1, :] = jnp.broadcast_to(jnp.sum(total, axis=1, keepdims=True), (1, LANES))


def forward_kernel(
    marks_ref, state_ref, depth_ref, lead_ref, table_t_ref, chip_ref, mine_ref, theirs_ref, weighted_ref, *,
    block, tau,
):
    coefs, sources = state_ref.shape
    own = mine_ref.shape[0] // 3
    first_core = marks_ref[1:2, 0:1] == 0
    start = marks_ref[0:1, 0:1]
    bounds = (start, start + GROUP)
    none = jnp.zeros((), BF16)
    for j in range(sources // block):
        cols = slice(j * block, (j + 1) * block)
        half = j * block // GROUP
        before = j * block + lax.broadcasted_iota(jnp.int32, (1, block), 1) < bounds[half]
        weighted = (state_ref[:, cols] * depth_ref[:, cols]).astype(BF16)
        inner = slice(j * block - half * GROUP, (j + 1) * block - half * GROUP)
        weighted_ref[half, :coefs, inner] = jnp.where(before, weighted, none)
        weighted_ref[half, coefs:, inner] = jnp.where(before, none, weighted)
    halves = [dot_t(weighted_ref[h], lead_ref[:, h * GROUP : (h + 1) * GROUP]) for h in range(2)]
    middle = group_scale(chip_ref[1:2, 0:1], tau) * (halves[0][coefs:] + halves[1][:coefs])
    parts = (halves[0][:coefs], middle, halves[1][coefs:])
    for g in range(3):
        samples = to_samples(table_t_ref, parts[g])
        front, back = samples[:own], samples[own:]
        theirs = jnp.where(first_core, back[:SPILL], front[:SPILL])
        mine_ref[g * own : (g + 1) * own, :] = jnp.where(first_core, front, back)
        theirs_ref[g * SPILL : (g + 1) * SPILL, :] = theirs.astype(BF16)


def fold_kernel(mine_ref, theirs_ref, *rest, tau):
    *powers, out_ref, scale_ref = rest
    own = out_ref.shape[0]
    scale_ref[...] = jnp.zeros_like(scale_ref)
    mine, theirs = 0.0, 0.0
    for g, scale in enumerate(scales_of(powers, tau)):
        scale_ref[g : g + 1, :] = scale
        by = 1.0 if g == 1 else scale[:, 0:1]
        mine += by * mine_ref[g * own : (g + 1) * own, :]
        theirs += by * theirs_ref[g * SPILL : (g + 1) * SPILL, :].astype(F32)
    out_ref[:SPILL] = (mine[:SPILL] + theirs).astype(BF16)
    out_ref[SPILL:] = mine[SPILL:].astype(BF16)


def plane_kernel(got_ref, out_ref):
    total = sum(slabs(got_ref[...].astype(F32)))
    out_ref[...] = jnp.concatenate([total] * (out_ref.shape[0] // 8), axis=0).astype(BF16)


def owner_kernel(got_ref, measured_ref, out_ref, *, last):
    row = measured_ref[...] - sum(slabs(got_ref[...].astype(F32)))
    if last:
        high = row.astype(BF16).astype(F32)
        row = jnp.concatenate([high, row - high], axis=0)
    out_ref[...] = jnp.concatenate([row] * (out_ref.shape[0] // row.shape[0]), axis=0).astype(BF16)


def add_kernel(a_ref, b_ref, out_ref):
    out_ref[...] = a_ref[...] + b_ref[...]


def residual_kernel(own_ref, out_ref):
    pieces = slabs(own_ref[...].astype(F32))
    rows = jnp.concatenate([high + low for high, low in zip(pieces[::2], pieces[1::2])], axis=0)
    for t in range(out_ref.shape[0] // LANES):
        lanes = slice(t * LANES, (t + 1) * LANES)
        out_ref[lanes, :] = rows[:, lanes].T


def estimate_kernel(marks_ref, state_ref, *rest, tau, middle):
    if middle:
        chip_ref, out_hbm, scaled_ref, sem = rest
        scales = [None, group_scale(chip_ref[1:2, 0:1], tau), None]
    else:
        *powers, _, out_hbm, scaled_ref, sem = rest
        scales = [scale[:, 0:1] for scale in scales_of(powers, tau)]
    blocks, _, block = scaled_ref.shape
    start = jnp.max(marks_ref[0:1, :])
    bounds = (start, start + GROUP)
    wanted, stores = [], []
    for j in range(blocks):
        cols = slice(j * block, (j + 1) * block)
        half = j * block // GROUP
        inside = bounds[0] <= j * block if half == 0 else (j + 1) * block <= bounds[1]
        wanted.append(inside if middle else jnp.logical_not(inside))
        stores.append(pltpu.make_async_copy(scaled_ref.at[j], out_hbm.at[:, cols], sem.at[j]))

        @pl.when(wanted[j])
        def _():
            if middle:
                scale = scales[1]
            else:
                before = j * block + lax.broadcasted_iota(jnp.int32, (1, block), 1) < bounds[half]
                scale = jnp.where(before, scales[half], scales[half + 1])
            scaled_ref[j] = state_ref[:, cols] * scale
            stores[j].start()

    for j in range(blocks):
        pl.when(wanted[j])(stores[j].wait)


SMEM = pl.BlockSpec(memory_space=pltpu.SMEM)
VMEM = pl.BlockSpec(memory_space=pltpu.VMEM)
HBM = pl.BlockSpec(memory_space=pltpu.HBM)


def struct(dtype, *shape):
    return jax.ShapeDtypeStruct(shape, dtype)


def call(kernel, name, args, outs, *, ins=None, out_specs=None, scratch=(), cost=None, alias=None):
    return pl.pallas_call(
        kernel, in_specs=ins or [VMEM] * len(args), out_specs=out_specs or [VMEM] * len(outs), out_shape=outs,
        scratch_shapes=list(scratch), compiler_params=PARAMS, name=name, cost_estimate=cost,
        input_output_aliases=alias or {},
    )(*args)


def stay(x):
    return pltpu.with_memory_space_constraint(x, pltpu.HBM)


def first_call(where, offsets, groups, depth, measured, state, lead):
    coefs, sources = state.shape
    sensors, own = measured.shape
    total = 2 * own
    dma = pltpu.SemaphoreType.DMA((sources // FIRST_BLOCK,))
    inputs = (offsets, jnp.asarray(windowed_cosines()), groups, depth, measured, state, lead)
    return call(
        first_kernel,
        "first_forward",
        [where] + [stay(x) for x in inputs],
        [
            struct(BF16, 2, coefs, total),
            struct(BF16, 2, total, coefs),
            struct(BF16, total, sensors),
            struct(jnp.int32, 8, LANES),
            struct(F32, 8, sensors),
            struct(F32, 1, sources),
            struct(F32, coefs, sources),
            struct(BF16, sensors, sources),
        ],
        ins=[SMEM] + [HBM] * len(inputs),
                scratch=[
            pltpu.SMEM(offsets.shape, jnp.int32),
            pltpu.VMEM((4, K, K), BF16),
            pltpu.VMEM((1, sources), jnp.int32),
            pltpu.VMEM((sensors, own), F32),
            pltpu.VMEM((own, sensors), F32),
            pltpu.VMEM((coefs, sensors), F32),
            dma,
            dma,
            pltpu.SemaphoreType.DMA((5,)),
        ],
    )


def step_call(marks, got, others, table, scale, depth, state, lead):
    coefs, sources = state.shape
    sensors = lead.shape[0]
    first, last = scale is None, others is not None
    args = [marks, got] + ([others] if last else []) + [table, depth, state, lead] + ([] if first else [scale])
    return call(
        lambda *refs: step_kernel(*refs, first=first, last=last, block=BLOCK),
        "step",
        args,
        [struct(F32, coefs, sources), struct(F32, 8, LANES)],
        scratch=[pltpu.VMEM((coefs, sensors), BF16)] + ([pltpu.VMEM((table.shape[2], sensors), BF16)] if last else []),
    )


def forward_call(marks, state, depth, lead, table_t, chip, tau):
    coefs, sources = state.shape
    sensors = lead.shape[0]
    own = table_t.shape[1] // 2
    return call(
        lambda *refs: forward_kernel(*refs, block=BLOCK, tau=tau),
        "forward",
        [marks, state, depth, lead, table_t, chip],
        [struct(F32, 3 * own, sensors), struct(BF16, 3 * SPILL, sensors)],
        scratch=[pltpu.VMEM((2, 2 * coefs, GROUP), BF16)],
        cost=pl.CostEstimate(flops=4 * coefs * sources * sensors, bytes_accessed=8 << 20, transcendentals=0),
    )


def estimate_call(marks, state, powers, tau, so_far=None):
    coefs, sources = state.shape
    blocks = sources // BLOCK
    middle = so_far is None
    args = [marks, state, *powers] + ([] if middle else [so_far])
    return call(
        lambda *refs: estimate_kernel(*refs, tau=tau, middle=middle),
        "estimate",
        args,
        [struct(F32, coefs, sources)],
        ins=[VMEM] * (2 + len(powers)) + ([] if middle else [HBM]),
        out_specs=[HBM],
        scratch=[pltpu.VMEM((blocks, coefs, BLOCK), F32), pltpu.SemaphoreType.DMA((blocks,))],
        alias={} if middle else {len(args) - 1: 0},
        cost=pl.CostEstimate(flops=coefs * sources, bytes_accessed=4 << 20, transcendentals=0),
    )[0]


def shards(measured, lead_field, depth, coefficients, offsets, group_ids):
    sensors, own = measured.shape
    sources = lead_field.shape[1]
    frames = coefficients.shape[1]
    frm_count = lax.axis_size("frm")
    src_count = math.prod(AXES.values())
    total = own * frm_count
    coefs = frames * K
    tau = group_weight * math.sqrt(GROUP * frames * frm_count * K)
    where = jnp.stack([lax.axis_index("frm"), lax.axis_index(PLANE)])

    def exchange(rows, axes):
        return lax.all_to_all(rows, axes, 0, 0, tiled=True)

    def move(x, chips, cores):
        route = []
        for chip in range(src_count):
            for core in range(frm_count):
                to = (chip + chips) % src_count * frm_count + (core + cores) % frm_count
                route.append((chip * frm_count + core, to))
        return lax.ppermute(x, (*SRC, "frm"), route)

    state = coefficients.transpose(1, 2, 0).reshape(coefs, sources)
    table, table_t, folded, marks, rows, depth_row, state, lead = first_call(
        where, offsets, group_ids.reshape(1, sources), depth.reshape(1, sources), measured, state, lead_field
    )
    scale = None
    for iteration in range(ITERS):
        last = iteration == ITERS - 1
        plane = call(
            plane_kernel, "plane_sum", [exchange(folded, PLANES if iteration == 0 else PLANE)], [struct(BF16, 8 * AXES["z"], sensors)]
        )[0]
        slab = call(
            lambda *refs, last=last: owner_kernel(*refs, last=last),
            "owner",
            [exchange(plane, "z"), rows],
            [struct(BF16, total, sensors)],
        )[0]
        got = exchange(slab, PLANE if last else PLANES)
        others = move(got, 0, 1) if last else None
        state, power = step_call(marks, got, others, table, scale, depth_row, state, lead)
        pair = move(power, 0, 1)
        chip = call(add_kernel, "chip_power", [power, pair], [struct(F32, 8, LANES)])[0]
        route = []
        for at in range(src_count):
            route.append((at * frm_count, (at + 1) % src_count * frm_count))
            route.append((at * frm_count + 1, (at - 1) % src_count * frm_count + 1))
        side = lax.ppermute(chip, (*SRC, "frm"), route)
        if last:
            residual = call(residual_kernel, "residual", [got], [struct(F32, sensors, own)])[0]
            estimate = estimate_call(marks, state, [chip], tau)
            side, residual, estimate = lax.optimization_barrier((side, residual, estimate))
            powers = [chip, side, move(side, 0, 1), marks]
        else:
            mine, theirs = forward_call(marks, state, depth_row, lead, table_t, chip, tau)
            theirs, side = lax.optimization_barrier((theirs, side))
            powers = [chip, side, move(side, 0, 1), marks]
        if not last:
            folded, scale = call(
                lambda *refs: fold_kernel(*refs, tau=tau),
                "fold",
                [mine, move(theirs, 0, 1), *powers],
                [struct(BF16, own, sensors), struct(F32, 8, LANES)],
            )

    estimate = estimate_call(marks, state, powers, tau, estimate)
    return (estimate.reshape(frames, K, sources).transpose(2, 0, 1), residual)


def solution(mesh):
    fine = Mesh(mesh.devices.reshape(*AXES.values(), mesh.shape["frm"]), (*AXES, "frm"))
    return jax.shard_map(
        shards,
        mesh=fine,
        in_specs=(
            P(None, "frm"),
            P(None, SRC),
            P(SRC),
            P(SRC, "frm", None),
            P("frm"),
            P(SRC),
        ),
        out_specs=(P(SRC, "frm", None), P(None, "frm")),
        check_vma=False,
    )
```

```python
import math

import jax
import jax.numpy as jnp
import ml_dtypes
import numpy as np
from jax import lax
from jax.experimental import pallas as pl
from jax.experimental.pallas import tpu as pltpu
from jax.sharding import Mesh
from jax.sharding import PartitionSpec as P

K = 64
GROUP = 2048
ITERS = 3
LANES = 128
BLOCK = 512
FIRST_BLOCK = 2048
SPILL = 64
step_size = 0.5
shrink_one = 0.05
group_weight = 0.03
epsilon = 1e-06

F32 = jnp.float32
BF16 = jnp.bfloat16
HIGHEST = lax.Precision.HIGHEST
PARAMS = pltpu.CompilerParams(vmem_limit_bytes=16 * 1024 * 1024)
AXES = {"x": 4, "z": 8, "y": 4}
SRC = ("x", "z", "y")
PLANE = ("x", "y")
PLANES = ("frm", "x", "y")


def windowed_cosines():
    t = np.arange(K)[:, None] + 0.5
    k = np.arange(K)[None, :] + 0.5
    wave = np.sin(np.pi * t / K) * np.sqrt(2.0 / K) * np.cos(np.pi * k * t / K)
    high = wave.astype(ml_dtypes.bfloat16)
    low = (wave - high.astype(np.float64)).astype(ml_dtypes.bfloat16)
    return np.stack([high, low, high.T, low.T])


def split(x):
    high = x.astype(BF16)
    return high, (x - high.astype(F32)).astype(BF16)


def dot(a, b):
    return jnp.dot(a, b, preferred_element_type=F32)


def dot_t(a, b):
    return lax.dot_general(a, b, (((1,), (1,)), ((), ())), preferred_element_type=F32)


def to_samples(atoms_ref, sums):
    high, low = split(sums)
    return dot(atoms_ref[0], high) + dot(atoms_ref[0], low) + dot(atoms_ref[1], high)


def group_scale(power, tau):
    return jnp.maximum(0.0, 1.0 - tau / jnp.sqrt(power + epsilon))


def scales_of(powers, tau):
    chip, *others = (ref[...] for ref in powers)
    if len(others) == 2:
        after, before = others
    else:
        one, two, marks = others
        first_core = marks[1:2, :] == 0
        before, after = jnp.where(first_core, one, two), jnp.where(first_core, two, one)
    return (
        group_scale(chip[0:1] + before[2:3], tau),
        group_scale(chip[1:2], tau),
        group_scale(chip[2:3] + after[0:1], tau),
    )


def first_kernel(
    where_ref, offsets_hbm, wave_hbm, group_hbm, depth_hbm, measured_hbm, coef_hbm, lead_hbm,
    table_ref, table_t_ref, out_ref, marks_ref, rows_ref, depth_ref, coef_ref, lead_ref,
    offsets_ref, wave_ref, group_ref, measured_ref, turned_ref, acc_ref, coef_sem, lead_sem, small_sem,
):
    total = table_ref.shape[2]
    sources = lead_ref.shape[1]
    blocks = lead_sem.shape[0]
    block = sources // blocks
    pairs = (
        (offsets_hbm, offsets_ref), (wave_hbm, wave_ref), (group_hbm, group_ref), (measured_hbm, measured_ref),
        (depth_hbm, depth_ref),
    )
    small = [pltpu.make_async_copy(a, b, small_sem.at[n]) for n, (a, b) in enumerate(pairs)]
    for load in small:
        load.start()
    loads = []
    for j in range(blocks):
        cols = slice(j * block, (j + 1) * block)
        loads.append(
            (
                pltpu.make_async_copy(lead_hbm.at[:, cols], lead_ref.at[:, cols], lead_sem.at[j]),
                pltpu.make_async_copy(coef_hbm.at[:, cols], coef_ref.at[:, cols], coef_sem.at[j]),
            )
        )
        for load in loads[-1]:
            load.start()
    for load in small:
        load.wait()

    groups = group_ref[...]
    edge = jnp.sum((groups == groups[0:1, 0:1]).astype(jnp.int32), axis=1, keepdims=True)
    marks_ref[0:1, :] = jnp.broadcast_to(edge, (1, LANES))
    marks_ref[1:2, :] = jnp.full((1, LANES), where_ref[0], jnp.int32)
    marks_ref[2:8, :] = jnp.zeros((6, LANES), jnp.int32)
    for t in range(measured_ref.shape[0] // LANES):
        lanes = slice(t * LANES, (t + 1) * LANES)
        turned_ref[:, lanes] = measured_ref[lanes, :].T
    rows_ref[...] = turned_ref[pl.ds(pl.multiple_of(where_ref[1] * 8, 8), 8), :]
    for f in range(offsets_ref.shape[0]):
        rows = slice(f * K, (f + 1) * K)
        for axis in range(2):
            shape = (total, K) if axis == 0 else (K, total)
            sample = lax.broadcasted_iota(jnp.int32, shape, axis)
            position = lax.broadcasted_iota(jnp.int32, shape, 1 - axis)
            delay = lax.rem(sample - offsets_ref[f] + total, total)
            placing = (delay == position).astype(F32).astype(BF16)
            for h in range(2):
                if axis == 0:
                    table_t_ref[h, :, rows] = dot(placing, wave_ref[h]).astype(BF16)
                else:
                    table_ref[h, rows, :] = dot(wave_ref[2 + h], placing).astype(BF16)

    for j in range(blocks):
        for load in loads[j]:
            load.wait()
        cols = slice(j * block, (j + 1) * block)
        part = dot_t((coef_ref[:, cols] * depth_ref[:, cols]).astype(BF16), lead_ref[:, cols])
        if j == 0:
            acc_ref[...] = part
        else:
            acc_ref[...] += part
    out_ref[...] = to_samples(table_t_ref, acc_ref[...]).astype(BF16)


def slabs(x):
    return [x[i : i + 8] for i in range(0, x.shape[0], 8)]


def step_kernel(
    marks_ref, got_ref, *rest, first, last, block
):
    other_ref, *rest = rest
    table_ref, depth_ref, state_ref, lead_ref, *rest = rest
    if not first:
        scale_ref, *rest = rest
    new_ref, power_ref, turned_ref, *rest = rest
    sources = state_ref.shape[1]
    (samples_ref,) = rest
    own = samples_ref.shape[0] // 2
    halves = [ref[...].astype(F32) for ref in (got_ref, other_ref)]
    if last:
        halves = [jnp.concatenate(slabs(half)[::2], axis=0) for half in halves]
    first_core = marks_ref[1:2, 0:1] == 0
    samples_ref[:own] = jnp.where(first_core, *halves).astype(BF16)
    samples_ref[own:] = jnp.where(first_core, *halves[::-1]).astype(BF16)
    turned = dot(table_ref[0], samples_ref[...]) + dot(table_ref[1], samples_ref[...])
    turned_ref[...] = turned.astype(BF16)

    start = marks_ref[0:1, 0:1]
    bounds = (start, start + GROUP)
    scales = None if first else [scale_ref[g : g + 1, 0:1] for g in range(3)]
    sums = [jnp.zeros((1, block), F32) for _ in range(4)]
    for j in range(sources // block):
        cols = slice(j * block, (j + 1) * block)
        half = j * block // GROUP
        gradient = dot(turned_ref[...], lead_ref[:, cols])
        source = j * block + lax.broadcasted_iota(jnp.int32, (1, block), 1)
        before = source < bounds[half]
        state = state_ref[:, cols]
        if not first:
            state = state * jnp.where(before, scales[half], scales[half + 1])
        moved = state + (step_size * depth_ref[:, cols]) * gradient
        shrunk = moved - jnp.clip(moved, -shrink_one, shrink_one)
        new_ref[:, cols] = shrunk
        squares = jnp.sum(shrunk * shrunk, axis=0, keepdims=True)
        sums[2 * half] += jnp.where(before, squares, 0.0)
        sums[2 * half + 1] += jnp.where(before, 0.0, squares)
    power_ref[...] = jnp.zeros_like(power_ref)
    for g, total in enumerate((sums[0], sums[1] + sums[2], sums[3])):
        power_ref[g : g + 1, :] = jnp.broadcast_to(jnp.sum(total, axis=1, keepdims=True), (1, LANES))


def forward_kernel(
    marks_ref, state_ref, depth_ref, lead_ref, table_t_ref, chip_ref, mine_ref, theirs_ref, weighted_ref, *,
    block, tau,
):
    coefs, sources = state_ref.shape
    own = mine_ref.shape[0] // 3
    first_core = marks_ref[1:2, 0:1] == 0
    start = marks_ref[0:1, 0:1]
    bounds = (start, start + GROUP)
    none = jnp.zeros((), BF16)
    for j in range(sources // block):
        cols = slice(j * block, (j + 1) * block)
        half = j * block // GROUP
        before = j * block + lax.broadcasted_iota(jnp.int32, (1, block), 1) < bounds[half]
        weighted = (state_ref[:, cols] * depth_ref[:, cols]).astype(BF16)
        inner = slice(j * block - half * GROUP, (j + 1) * block - half * GROUP)
        weighted_ref[half, :coefs, inner] = jnp.where(before, weighted, none)
        weighted_ref[half, coefs:, inner] = jnp.where(before, none, weighted)
    halves = [dot_t(weighted_ref[h], lead_ref[:, h * GROUP : (h + 1) * GROUP]) for h in range(2)]
    middle = group_scale(chip_ref[1:2, 0:1], tau) * (halves[0][coefs:] + halves[1][:coefs])
    parts = (halves[0][:coefs], middle, halves[1][coefs:])
    for g in range(3):
        samples = to_samples(table_t_ref, parts[g])
        front, back = samples[:own], samples[own:]
        theirs = jnp.where(first_core, back[:SPILL], front[:SPILL])
        mine_ref[g * own : (g + 1) * own, :] = jnp.where(first_core, front, back)
        theirs_ref[g * SPILL : (g + 1) * SPILL, :] = theirs.astype(BF16)


def fold_kernel(mine_ref, theirs_ref, *rest, tau):
    *powers, out_ref, scale_ref = rest
    own = out_ref.shape[0]
    scale_ref[...] = jnp.zeros_like(scale_ref)
    mine, theirs = 0.0, 0.0
    for g, scale in enumerate(scales_of(powers, tau)):
        scale_ref[g : g + 1, :] = scale
        by = 1.0 if g == 1 else scale[:, 0:1]
        mine += by * mine_ref[g * own : (g + 1) * own, :]
        theirs += by * theirs_ref[g * SPILL : (g + 1) * SPILL, :].astype(F32)
    out_ref[:SPILL] = (mine[:SPILL] + theirs).astype(BF16)
    out_ref[SPILL:] = mine[SPILL:].astype(BF16)


def plane_kernel(got_ref, out_ref):
    total = sum(slabs(got_ref[...].astype(F32)))
    out_ref[...] = jnp.concatenate([total] * (out_ref.shape[0] // 8), axis=0).astype(BF16)


def owner_kernel(got_ref, measured_ref, out_ref, *, last):
    row = measured_ref[...] - sum(slabs(got_ref[...].astype(F32)))
    if last:
        high = row.astype(BF16).astype(F32)
        row = jnp.concatenate([high, row - high], axis=0)
    out_ref[...] = jnp.concatenate([row] * (out_ref.shape[0] // row.shape[0]), axis=0).astype(BF16)


def add_kernel(a_ref, b_ref, out_ref):
    out_ref[...] = a_ref[...] + b_ref[...]


def residual_kernel(own_ref, out_ref):
    pieces = slabs(own_ref[...].astype(F32))
    rows = jnp.concatenate([high + low for high, low in zip(pieces[::2], pieces[1::2])], axis=0)
    for t in range(out_ref.shape[0] // LANES):
        lanes = slice(t * LANES, (t + 1) * LANES)
        out_ref[lanes, :] = rows[:, lanes].T


def estimate_kernel(marks_ref, state_ref, *rest, tau, middle):
    if middle:
        chip_ref, out_hbm, scaled_ref, sem = rest
        scales = [None, group_scale(chip_ref[1:2, 0:1], tau), None]
    else:
        *powers, _, out_hbm, scaled_ref, sem = rest
        scales = [scale[:, 0:1] for scale in scales_of(powers, tau)]
    blocks, _, block = scaled_ref.shape
    start = jnp.max(marks_ref[0:1, :])
    bounds = (start, start + GROUP)
    wanted, stores = [], []
    for j in range(blocks):
        cols = slice(j * block, (j + 1) * block)
        half = j * block // GROUP
        inside = bounds[0] <= j * block if half == 0 else (j + 1) * block <= bounds[1]
        wanted.append(inside if middle else jnp.logical_not(inside))
        stores.append(pltpu.make_async_copy(scaled_ref.at[j], out_hbm.at[:, cols], sem.at[j]))

        @pl.when(wanted[j])
        def _():
            if middle:
                scale = scales[1]
            else:
                before = j * block + lax.broadcasted_iota(jnp.int32, (1, block), 1) < bounds[half]
                scale = jnp.where(before, scales[half], scales[half + 1])
            scaled_ref[j] = state_ref[:, cols] * scale
            stores[j].start()

    for j in range(blocks):
        pl.when(wanted[j])(stores[j].wait)


SMEM = pl.BlockSpec(memory_space=pltpu.SMEM)
VMEM = pl.BlockSpec(memory_space=pltpu.VMEM)
HBM = pl.BlockSpec(memory_space=pltpu.HBM)


def struct(dtype, *shape):
    return jax.ShapeDtypeStruct(shape, dtype)


def call(kernel, name, args, outs, *, ins=None, out_specs=None, scratch=(), cost=None, alias=None):
    return pl.pallas_call(
        kernel, in_specs=ins or [VMEM] * len(args), out_specs=out_specs or [VMEM] * len(outs), out_shape=outs,
        scratch_shapes=list(scratch), compiler_params=PARAMS, name=name, cost_estimate=cost,
        input_output_aliases=alias or {},
    )(*args)


def stay(x):
    return pltpu.with_memory_space_constraint(x, pltpu.HBM)


def first_call(where, offsets, groups, depth, measured, state, lead):
    coefs, sources = state.shape
    sensors, own = measured.shape
    total = 2 * own
    dma = pltpu.SemaphoreType.DMA((sources // FIRST_BLOCK,))
    inputs = (offsets, jnp.asarray(windowed_cosines()), groups, depth, measured, state, lead)
    return call(
        first_kernel,
        "first_forward",
        [where] + [stay(x) for x in inputs],
        [
            struct(BF16, 2, coefs, total),
            struct(BF16, 2, total, coefs),
            struct(BF16, total, sensors),
            struct(jnp.int32, 8, LANES),
            struct(F32, 8, sensors),
            struct(F32, 1, sources),
            struct(F32, coefs, sources),
            struct(BF16, sensors, sources),
        ],
        ins=[SMEM] + [HBM] * len(inputs),
                scratch=[
            pltpu.SMEM(offsets.shape, jnp.int32),
            pltpu.VMEM((4, K, K), BF16),
            pltpu.VMEM((1, sources), jnp.int32),
            pltpu.VMEM((sensors, own), F32),
            pltpu.VMEM((own, sensors), F32),
            pltpu.VMEM((coefs, sensors), F32),
            dma,
            dma,
            pltpu.SemaphoreType.DMA((5,)),
        ],
    )


def step_call(marks, got, others, table, scale, depth, state, lead, last):
    coefs, sources = state.shape
    sensors = lead.shape[0]
    first = scale is None
    args = [marks, got, others, table, depth, state, lead] + ([] if first else [scale])
    return call(
        lambda *refs: step_kernel(*refs, first=first, last=last, block=BLOCK),
        "step",
        args,
        [struct(F32, coefs, sources), struct(F32, 8, LANES)],
        scratch=[pltpu.VMEM((coefs, sensors), BF16), pltpu.VMEM((table.shape[2], sensors), BF16)],
    )


def forward_call(marks, state, depth, lead, table_t, chip, tau):
    coefs, sources = state.shape
    sensors = lead.shape[0]
    own = table_t.shape[1] // 2
    return call(
        lambda *refs: forward_kernel(*refs, block=BLOCK, tau=tau),
        "forward",
        [marks, state, depth, lead, table_t, chip],
        [struct(F32, 3 * own, sensors), struct(BF16, 3 * SPILL, sensors)],
        scratch=[pltpu.VMEM((2, 2 * coefs, GROUP), BF16)],
        cost=pl.CostEstimate(flops=4 * coefs * sources * sensors, bytes_accessed=8 << 20, transcendentals=0),
    )


def estimate_call(marks, state, powers, tau, so_far=None):
    coefs, sources = state.shape
    blocks = sources // BLOCK
    middle = so_far is None
    args = [marks, state, *powers] + ([] if middle else [so_far])
    return call(
        lambda *refs: estimate_kernel(*refs, tau=tau, middle=middle),
        "estimate",
        args,
        [struct(F32, coefs, sources)],
        ins=[VMEM] * (2 + len(powers)) + ([] if middle else [HBM]),
        out_specs=[HBM],
        scratch=[pltpu.VMEM((blocks, coefs, BLOCK), F32), pltpu.SemaphoreType.DMA((blocks,))],
        alias={} if middle else {len(args) - 1: 0},
        cost=pl.CostEstimate(flops=coefs * sources, bytes_accessed=4 << 20, transcendentals=0),
    )[0]


def shards(measured, lead_field, depth, coefficients, offsets, group_ids):
    sensors, own = measured.shape
    sources = lead_field.shape[1]
    frames = coefficients.shape[1]
    frm_count = lax.axis_size("frm")
    src_count = math.prod(AXES.values())
    total = own * frm_count
    coefs = frames * K
    tau = group_weight * math.sqrt(GROUP * frames * frm_count * K)
    where = jnp.stack([lax.axis_index("frm"), lax.axis_index(PLANE)])

    def exchange(rows, axes):
        return lax.all_to_all(rows, axes, 0, 0, tiled=True)

    def move(x, chips, cores):
        route = []
        for chip in range(src_count):
            for core in range(frm_count):
                to = (chip + chips) % src_count * frm_count + (core + cores) % frm_count
                route.append((chip * frm_count + core, to))
        return lax.ppermute(x, (*SRC, "frm"), route)

    opposite = []
    for chip in range(src_count):
        opposite.append((chip * frm_count, (chip + 1) % src_count * frm_count))
        opposite.append((chip * frm_count + 1, (chip - 1) % src_count * frm_count + 1))

    state = coefficients.transpose(1, 2, 0).reshape(coefs, sources)
    table, table_t, folded, marks, rows, depth_row, state, lead = first_call(
        where, offsets, group_ids.reshape(1, sources), depth.reshape(1, sources), measured, state, lead_field
    )
    scale = None
    for iteration in range(ITERS):
        last = iteration == ITERS - 1
        plane = call(
            plane_kernel, "plane_sum", [exchange(folded, PLANES if iteration == 0 else PLANE)], [struct(BF16, 8 * AXES["z"], sensors)]
        )[0]
        slab = call(
            lambda *refs, last=last: owner_kernel(*refs, last=last),
            "owner",
            [exchange(plane, "z"), rows],
            [struct(BF16, total if last else own, sensors)],
        )[0]
        got = exchange(slab, PLANE)
        state, power = step_call(
            marks, got, move(got, 0, 1), table, scale, depth_row, state, lead, last
        )
        pair = move(power, 0, 1)
        chip = call(add_kernel, "chip_power", [power, pair], [struct(F32, 8, LANES)])[0]
        if last:
            residual = call(residual_kernel, "residual", [got], [struct(F32, sensors, own)])[0]
            estimate = estimate_call(marks, state, [chip], tau)
            powers = [chip, move(chip, -1, 0), move(chip, 1, 0)]
        else:
            mine, theirs = forward_call(marks, state, depth_row, lead, table_t, chip, tau)
            side = lax.ppermute(chip, (*SRC, "frm"), opposite)
            theirs, side = lax.optimization_barrier((theirs, side))
            powers = [chip, side, move(side, 0, 1), marks]
        if not last:
            folded, scale = call(
                lambda *refs: fold_kernel(*refs, tau=tau),
                "fold",
                [mine, move(theirs, 0, 1), *powers],
                [struct(BF16, own, sensors), struct(F32, 8, LANES)],
            )

    estimate = estimate_call(marks, state, powers, tau, estimate)
    return (estimate.reshape(frames, K, sources).transpose(2, 0, 1), residual)


def solution(mesh):
    fine = Mesh(mesh.devices.reshape(*AXES.values(), mesh.shape["frm"]), (*AXES, "frm"))
    return jax.shard_map(
        shards,
        mesh=fine,
        in_specs=(
            P(None, "frm"),
            P(None, SRC),
            P(SRC),
            P(SRC, "frm", None),
            P("frm"),
            P(SRC),
        ),
        out_specs=(P(SRC, "frm", None), P(None, "frm")),
        check_vma=False,
    )
```

```python
import math

import jax
import jax.numpy as jnp
import ml_dtypes
import numpy as np
from jax import lax
from jax.experimental import pallas as pl
from jax.experimental.pallas import tpu as pltpu
from jax.sharding import Mesh
from jax.sharding import PartitionSpec as P

K = 64
GROUP = 2048
ITERS = 3
LANES = 128
BLOCK = 512
FIRST_BLOCK = 4096
SPILL = 64
step_size = 0.5
shrink_one = 0.05
group_weight = 0.03
epsilon = 1e-06

F32 = jnp.float32
BF16 = jnp.bfloat16
HIGHEST = lax.Precision.HIGHEST
PARAMS = pltpu.CompilerParams(vmem_limit_bytes=16 * 1024 * 1024)
AXES = {"x": 4, "z": 8, "y": 4}
SRC = ("x", "z", "y")
PLANE = ("x", "y")
PLANES = ("frm", "x", "y")


def windowed_cosines():
    t = np.arange(K)[:, None] + 0.5
    k = np.arange(K)[None, :] + 0.5
    wave = np.sin(np.pi * t / K) * np.sqrt(2.0 / K) * np.cos(np.pi * k * t / K)
    high = wave.astype(ml_dtypes.bfloat16)
    low = (wave - high.astype(np.float64)).astype(ml_dtypes.bfloat16)
    return np.stack([high, low, high.T, low.T])


def split(x):
    high = x.astype(BF16)
    return high, (x - high.astype(F32)).astype(BF16)


def dot(a, b):
    return jnp.dot(a, b, preferred_element_type=F32)


def dot_t(a, b):
    return lax.dot_general(a, b, (((1,), (1,)), ((), ())), preferred_element_type=F32)


def to_samples(atoms_ref, sums):
    high, low = split(sums)
    return dot(atoms_ref[0], high) + dot(atoms_ref[0], low) + dot(atoms_ref[1], high)


def group_scale(power, tau):
    return jnp.maximum(0.0, 1.0 - tau / jnp.sqrt(power + epsilon))


def scales_of(powers, tau):
    chip, *others = (ref[...] for ref in powers)
    if len(others) == 2:
        after, before = others
    else:
        one, two, marks = others
        first_core = marks[1:2, :] == 0
        before, after = jnp.where(first_core, one, two), jnp.where(first_core, two, one)
    return (
        group_scale(chip[0:1] + before[2:3], tau),
        group_scale(chip[1:2], tau),
        group_scale(chip[2:3] + after[0:1], tau),
    )


def first_kernel(
    where_ref, offsets_hbm, wave_hbm, group_hbm, depth_hbm, measured_hbm, coef_hbm, lead_hbm,
    table_ref, table_t_ref, out_ref, marks_ref, rows_ref, depth_ref, coef_ref, lead_ref,
    offsets_ref, wave_ref, group_ref, measured_ref, turned_ref, acc_ref, coef_sem, lead_sem, small_sem,
):
    total = table_ref.shape[2]
    sources = lead_ref.shape[1]
    blocks = lead_sem.shape[0]
    block = sources // blocks
    pairs = (
        (offsets_hbm, offsets_ref), (wave_hbm, wave_ref), (group_hbm, group_ref), (measured_hbm, measured_ref),
        (depth_hbm, depth_ref),
    )
    small = [pltpu.make_async_copy(a, b, small_sem.at[n]) for n, (a, b) in enumerate(pairs)]
    for load in small:
        load.start()
    loads = []
    for j in range(blocks):
        cols = slice(j * block, (j + 1) * block)
        loads.append(
            (
                pltpu.make_async_copy(lead_hbm.at[:, cols], lead_ref.at[:, cols], lead_sem.at[j]),
                pltpu.make_async_copy(coef_hbm.at[:, cols], coef_ref.at[:, cols], coef_sem.at[j]),
            )
        )
        for load in loads[-1]:
            load.start()
    for load in small:
        load.wait()

    groups = group_ref[...]
    edge = jnp.sum((groups == groups[0:1, 0:1]).astype(jnp.int32), axis=1, keepdims=True)
    marks_ref[0:1, :] = jnp.broadcast_to(edge, (1, LANES))
    marks_ref[1:2, :] = jnp.full((1, LANES), where_ref[0], jnp.int32)
    marks_ref[2:8, :] = jnp.zeros((6, LANES), jnp.int32)
    for t in range(measured_ref.shape[0] // LANES):
        lanes = slice(t * LANES, (t + 1) * LANES)
        turned_ref[:, lanes] = measured_ref[lanes, :].T
    rows_ref[...] = turned_ref[pl.ds(pl.multiple_of(where_ref[1] * 8, 8), 8), :]
    for f in range(offsets_ref.shape[0]):
        rows = slice(f * K, (f + 1) * K)
        for axis in range(2):
            shape = (total, K) if axis == 0 else (K, total)
            sample = lax.broadcasted_iota(jnp.int32, shape, axis)
            position = lax.broadcasted_iota(jnp.int32, shape, 1 - axis)
            delay = lax.rem(sample - offsets_ref[f] + total, total)
            placing = (delay == position).astype(F32).astype(BF16)
            for h in range(2):
                if axis == 0:
                    table_t_ref[h, :, rows] = dot(placing, wave_ref[h]).astype(BF16)
                else:
                    table_ref[h, rows, :] = dot(wave_ref[2 + h], placing).astype(BF16)

    for j in range(blocks):
        for load in loads[j]:
            load.wait()
        cols = slice(j * block, (j + 1) * block)
        part = dot_t((coef_ref[:, cols] * depth_ref[:, cols]).astype(BF16), lead_ref[:, cols])
        if j == 0:
            acc_ref[...] = part
        else:
            acc_ref[...] += part
    out_ref[...] = to_samples(table_t_ref, acc_ref[...]).astype(BF16)


def slabs(x):
    return [x[i : i + 8] for i in range(0, x.shape[0], 8)]


def step_kernel(
    marks_ref, got_ref, *rest, first, last, block
):
    other_ref, *rest = rest
    table_ref, depth_ref, state_ref, lead_ref, *rest = rest
    if not first:
        scale_ref, *rest = rest
    new_ref, power_ref, turned_ref, *rest = rest
    sources = state_ref.shape[1]
    (samples_ref,) = rest
    own = samples_ref.shape[0] // 2
    halves = [ref[...].astype(F32) for ref in (got_ref, other_ref)]
    if last:
        halves = [jnp.concatenate(slabs(half)[::2], axis=0) for half in halves]
    first_core = marks_ref[1:2, 0:1] == 0
    samples_ref[:own] = jnp.where(first_core, *halves).astype(BF16)
    samples_ref[own:] = jnp.where(first_core, *halves[::-1]).astype(BF16)
    turned = dot(table_ref[0], samples_ref[...]) + dot(table_ref[1], samples_ref[...])
    turned_ref[...] = turned.astype(BF16)

    start = marks_ref[0:1, 0:1]
    bounds = (start, start + GROUP)
    scales = None if first else [scale_ref[g : g + 1, 0:1] for g in range(3)]
    sums = [jnp.zeros((1, block), F32) for _ in range(4)]
    for j in range(sources // block):
        cols = slice(j * block, (j + 1) * block)
        half = j * block // GROUP
        gradient = dot(turned_ref[...], lead_ref[:, cols])
        source = j * block + lax.broadcasted_iota(jnp.int32, (1, block), 1)
        before = source < bounds[half]
        state = state_ref[:, cols]
        if not first:
            state = state * jnp.where(before, scales[half], scales[half + 1])
        moved = state + (step_size * depth_ref[:, cols]) * gradient
        shrunk = moved - jnp.clip(moved, -shrink_one, shrink_one)
        new_ref[:, cols] = shrunk
        squares = jnp.sum(shrunk * shrunk, axis=0, keepdims=True)
        sums[2 * half] += jnp.where(before, squares, 0.0)
        sums[2 * half + 1] += jnp.where(before, 0.0, squares)
    power_ref[...] = jnp.zeros_like(power_ref)
    for g, total in enumerate((sums[0], sums[1] + sums[2], sums[3])):
        power_ref[g : g + 1, :] = jnp.broadcast_to(jnp.sum(total, axis=1, keepdims=True), (1, LANES))


def forward_kernel(
    marks_ref, state_ref, depth_ref, lead_ref, table_t_ref, chip_ref, mine_ref, theirs_ref, weighted_ref, *,
    block, tau,
):
    coefs, sources = state_ref.shape
    own = mine_ref.shape[0] // 3
    first_core = marks_ref[1:2, 0:1] == 0
    start = marks_ref[0:1, 0:1]
    bounds = (start, start + GROUP)
    none = jnp.zeros((), BF16)
    for j in range(sources // block):
        cols = slice(j * block, (j + 1) * block)
        half = j * block // GROUP
        before = j * block + lax.broadcasted_iota(jnp.int32, (1, block), 1) < bounds[half]
        weighted = (state_ref[:, cols] * depth_ref[:, cols]).astype(BF16)
        inner = slice(j * block - half * GROUP, (j + 1) * block - half * GROUP)
        weighted_ref[half, :coefs, inner] = jnp.where(before, weighted, none)
        weighted_ref[half, coefs:, inner] = jnp.where(before, none, weighted)
    halves = [dot_t(weighted_ref[h], lead_ref[:, h * GROUP : (h + 1) * GROUP]) for h in range(2)]
    middle = group_scale(chip_ref[1:2, 0:1], tau) * (halves[0][coefs:] + halves[1][:coefs])
    parts = (halves[0][:coefs], middle, halves[1][coefs:])
    for g in range(3):
        samples = to_samples(table_t_ref, parts[g])
        front, back = samples[:own], samples[own:]
        theirs = jnp.where(first_core, back[:SPILL], front[:SPILL])
        mine_ref[g * own : (g + 1) * own, :] = jnp.where(first_core, front, back)
        theirs_ref[g * SPILL : (g + 1) * SPILL, :] = theirs.astype(BF16)


def fold_kernel(mine_ref, theirs_ref, *rest, tau):
    *powers, out_ref, scale_ref = rest
    own = out_ref.shape[0]
    scale_ref[...] = jnp.zeros_like(scale_ref)
    mine, theirs = 0.0, 0.0
    for g, scale in enumerate(scales_of(powers, tau)):
        scale_ref[g : g + 1, :] = scale
        by = 1.0 if g == 1 else scale[:, 0:1]
        mine += by * mine_ref[g * own : (g + 1) * own, :]
        theirs += by * theirs_ref[g * SPILL : (g + 1) * SPILL, :].astype(F32)
    out_ref[:SPILL] = (mine[:SPILL] + theirs).astype(BF16)
    out_ref[SPILL:] = mine[SPILL:].astype(BF16)


def plane_kernel(got_ref, out_ref):
    total = sum(slabs(got_ref[...].astype(F32)))
    out_ref[...] = jnp.concatenate([total] * (out_ref.shape[0] // 8), axis=0).astype(BF16)


def owner_kernel(got_ref, measured_ref, out_ref, *, last):
    row = measured_ref[...] - sum(slabs(got_ref[...].astype(F32)))
    if last:
        high = row.astype(BF16).astype(F32)
        row = jnp.concatenate([high, row - high], axis=0)
    out_ref[...] = jnp.concatenate([row] * (out_ref.shape[0] // row.shape[0]), axis=0).astype(BF16)


def add_kernel(a_ref, b_ref, out_ref):
    out_ref[...] = a_ref[...] + b_ref[...]


def residual_kernel(own_ref, out_ref):
    pieces = slabs(own_ref[...].astype(F32))
    rows = jnp.concatenate([high + low for high, low in zip(pieces[::2], pieces[1::2])], axis=0)
    for t in range(out_ref.shape[0] // LANES):
        lanes = slice(t * LANES, (t + 1) * LANES)
        out_ref[lanes, :] = rows[:, lanes].T


def estimate_kernel(marks_ref, state_ref, *rest, tau, middle):
    if middle:
        chip_ref, out_hbm, scaled_ref, sem = rest
        scales = [None, group_scale(chip_ref[1:2, 0:1], tau), None]
    else:
        *powers, _, out_hbm, scaled_ref, sem = rest
        scales = [scale[:, 0:1] for scale in scales_of(powers, tau)]
    blocks, _, block = scaled_ref.shape
    start = jnp.max(marks_ref[0:1, :])
    bounds = (start, start + GROUP)
    wanted, stores = [], []
    for j in range(blocks):
        cols = slice(j * block, (j + 1) * block)
        half = j * block // GROUP
        inside = bounds[0] <= j * block if half == 0 else (j + 1) * block <= bounds[1]
        wanted.append(inside if middle else jnp.logical_not(inside))
        stores.append(pltpu.make_async_copy(scaled_ref.at[j], out_hbm.at[:, cols], sem.at[j]))

        @pl.when(wanted[j])
        def _():
            if middle:
                scale = scales[1]
            else:
                before = j * block + lax.broadcasted_iota(jnp.int32, (1, block), 1) < bounds[half]
                scale = jnp.where(before, scales[half], scales[half + 1])
            scaled_ref[j] = state_ref[:, cols] * scale
            stores[j].start()

    for j in range(blocks):
        pl.when(wanted[j])(stores[j].wait)


SMEM = pl.BlockSpec(memory_space=pltpu.SMEM)
VMEM = pl.BlockSpec(memory_space=pltpu.VMEM)
HBM = pl.BlockSpec(memory_space=pltpu.HBM)


def struct(dtype, *shape):
    return jax.ShapeDtypeStruct(shape, dtype)


def call(kernel, name, args, outs, *, ins=None, out_specs=None, scratch=(), cost=None, alias=None):
    return pl.pallas_call(
        kernel, in_specs=ins or [VMEM] * len(args), out_specs=out_specs or [VMEM] * len(outs), out_shape=outs,
        scratch_shapes=list(scratch), compiler_params=PARAMS, name=name, cost_estimate=cost,
        input_output_aliases=alias or {},
    )(*args)


def stay(x):
    return pltpu.with_memory_space_constraint(x, pltpu.HBM)


def first_call(where, offsets, groups, depth, measured, state, lead):
    coefs, sources = state.shape
    sensors, own = measured.shape
    total = 2 * own
    dma = pltpu.SemaphoreType.DMA((sources // FIRST_BLOCK,))
    inputs = (offsets, jnp.asarray(windowed_cosines()), groups, depth, measured, state, lead)
    return call(
        first_kernel,
        "first_forward",
        [where] + [stay(x) for x in inputs],
        [
            struct(BF16, 2, coefs, total),
            struct(BF16, 2, total, coefs),
            struct(BF16, total, sensors),
            struct(jnp.int32, 8, LANES),
            struct(F32, 8, sensors),
            struct(F32, 1, sources),
            struct(F32, coefs, sources),
            struct(BF16, sensors, sources),
        ],
        ins=[SMEM] + [HBM] * len(inputs),
                scratch=[
            pltpu.SMEM(offsets.shape, jnp.int32),
            pltpu.VMEM((4, K, K), BF16),
            pltpu.VMEM((1, sources), jnp.int32),
            pltpu.VMEM((sensors, own), F32),
            pltpu.VMEM((own, sensors), F32),
            pltpu.VMEM((coefs, sensors), F32),
            dma,
            dma,
            pltpu.SemaphoreType.DMA((5,)),
        ],
    )


def step_call(marks, got, others, table, scale, depth, state, lead, last):
    coefs, sources = state.shape
    sensors = lead.shape[0]
    first = scale is None
    args = [marks, got, others, table, depth, state, lead] + ([] if first else [scale])
    return call(
        lambda *refs: step_kernel(*refs, first=first, last=last, block=BLOCK),
        "step",
        args,
        [struct(F32, coefs, sources), struct(F32, 8, LANES)],
        scratch=[pltpu.VMEM((coefs, sensors), BF16), pltpu.VMEM((table.shape[2], sensors), BF16)],
    )


def forward_call(marks, state, depth, lead, table_t, chip, tau):
    coefs, sources = state.shape
    sensors = lead.shape[0]
    own = table_t.shape[1] // 2
    return call(
        lambda *refs: forward_kernel(*refs, block=BLOCK, tau=tau),
        "forward",
        [marks, state, depth, lead, table_t, chip],
        [struct(F32, 3 * own, sensors), struct(BF16, 3 * SPILL, sensors)],
        scratch=[pltpu.VMEM((2, 2 * coefs, GROUP), BF16)],
        cost=pl.CostEstimate(flops=4 * coefs * sources * sensors, bytes_accessed=8 << 20, transcendentals=0),
    )


def estimate_call(marks, state, powers, tau, so_far=None):
    coefs, sources = state.shape
    blocks = sources // BLOCK
    middle = so_far is None
    args = [marks, state, *powers] + ([] if middle else [so_far])
    return call(
        lambda *refs: estimate_kernel(*refs, tau=tau, middle=middle),
        "estimate",
        args,
        [struct(F32, coefs, sources)],
        ins=[VMEM] * (2 + len(powers)) + ([] if middle else [HBM]),
        out_specs=[HBM],
        scratch=[pltpu.VMEM((blocks, coefs, BLOCK), F32), pltpu.SemaphoreType.DMA((blocks,))],
        alias={} if middle else {len(args) - 1: 0},
        cost=pl.CostEstimate(flops=coefs * sources, bytes_accessed=4 << 20, transcendentals=0),
    )[0]


def shards(measured, lead_field, depth, coefficients, offsets, group_ids):
    sensors, own = measured.shape
    sources = lead_field.shape[1]
    frames = coefficients.shape[1]
    frm_count = lax.axis_size("frm")
    src_count = math.prod(AXES.values())
    total = own * frm_count
    coefs = frames * K
    tau = group_weight * math.sqrt(GROUP * frames * frm_count * K)
    where = jnp.stack([lax.axis_index("frm"), lax.axis_index(PLANE)])

    def exchange(rows, axes):
        return lax.all_to_all(rows, axes, 0, 0, tiled=True)

    def move(x, chips, cores):
        route = []
        for chip in range(src_count):
            for core in range(frm_count):
                to = (chip + chips) % src_count * frm_count + (core + cores) % frm_count
                route.append((chip * frm_count + core, to))
        return lax.ppermute(x, (*SRC, "frm"), route)

    opposite = []
    for chip in range(src_count):
        opposite.append((chip * frm_count, (chip + 1) % src_count * frm_count))
        opposite.append((chip * frm_count + 1, (chip - 1) % src_count * frm_count + 1))

    state = coefficients.transpose(1, 2, 0).reshape(coefs, sources)
    table, table_t, folded, marks, rows, depth_row, state, lead = first_call(
        where, offsets, group_ids.reshape(1, sources), depth.reshape(1, sources), measured, state, lead_field
    )
    scale = None
    for iteration in range(ITERS):
        last = iteration == ITERS - 1
        plane = call(
            plane_kernel, "plane_sum", [exchange(folded, PLANES if iteration == 0 else PLANE)], [struct(BF16, 8 * AXES["z"], sensors)]
        )[0]
        slab = call(
            lambda *refs, last=last: owner_kernel(*refs, last=last),
            "owner",
            [exchange(plane, "z"), rows],
            [struct(BF16, total if last else own, sensors)],
        )[0]
        got = exchange(slab, PLANE)
        state, power = step_call(
            marks, got, move(got, 0, 1), table, scale, depth_row, state, lead, last
        )
        pair = move(power, 0, 1)
        chip = call(add_kernel, "chip_power", [power, pair], [struct(F32, 8, LANES)])[0]
        if last:
            residual = call(residual_kernel, "residual", [got], [struct(F32, sensors, own)])[0]
            estimate = estimate_call(marks, state, [chip], tau)
            powers = [chip, move(chip, -1, 0), move(chip, 1, 0)]
        else:
            mine, theirs = forward_call(marks, state, depth_row, lead, table_t, chip, tau)
            side = lax.ppermute(chip, (*SRC, "frm"), opposite)
            theirs, side = lax.optimization_barrier((theirs, side))
            powers = [chip, side, move(side, 0, 1), marks]
        if not last:
            folded, scale = call(
                lambda *refs: fold_kernel(*refs, tau=tau),
                "fold",
                [mine, move(theirs, 0, 1), *powers],
                [struct(BF16, own, sensors), struct(F32, 8, LANES)],
            )

    estimate = estimate_call(marks, state, powers, tau, estimate)
    return (estimate.reshape(frames, K, sources).transpose(2, 0, 1), residual)


def solution(mesh):
    fine = Mesh(mesh.devices.reshape(*AXES.values(), mesh.shape["frm"]), (*AXES, "frm"))
    return jax.shard_map(
        shards,
        mesh=fine,
        in_specs=(
            P(None, "frm"),
            P(None, SRC),
            P(SRC),
            P(SRC, "frm", None),
            P("frm"),
            P(SRC),
        ),
        out_specs=(P(SRC, "frm", None), P(None, "frm")),
        check_vma=False,
    )
```
